256 devices in a mesh: noise: 8 (over x, core), dp: 32 (over y, z).
Axes of the slice: x: 4, y: 4, z: 8, core: 2. Of those that a mesh axis runs over, the one named last changes fastest.
Arguments:
- noise_latents: bfloat16 [32768, 128], P('noise'), may hold values from -6 to 6
- data_latents: bfloat16 [65536, 128], P('dp'), may hold values from -6 to 6
- projection: bfloat16 [128, 64], replicated, may hold values from -0.5 to 0.5
Outputs:
- targets: float32 [32768, 128], P(('noise', 'dp'))
- data_side_potential: float32 [65536], P('dp')
The draws below stay inside these ranges and needn't reach their ends.
All inputs are finite; a program needn't handle non-finite values.
Results may differ from the reference program's by a relative error of at most 0.015.
The reference program's roundings to bfloat16 on the way count: a program that leaves them out, or rounds other values in their place, can miss the bound.
Values sent between devices are 32-bit elements; how exact they have to be, the bound alone decides.
A program may use at most 192 MiB of HBM per device.

```python
import math
import jax
import jax.numpy as jnp
from jax import lax

D = 128
K = 64
C_DEV = 2048
NR = 32768
NC = 65536
N_DP = 32


def steps_of(key, extent, cuts, least, largest):
    gain, own = 1.0, jax.random.fold_in(key, 6)
    for position, shards_of in cuts:
        steps = jnp.exp(jax.random.uniform(jax.random.fold_in(own, position), (shards_of,), jnp.float32, least / len(cuts), largest / len(cuts)))
        gain = gain * jnp.repeat(steps, extent[position] // shards_of).reshape([-1 if axis == position else 1 for axis in range(len(extent))])
    return gain


def bell_draw(stream_key, dims, deviation, limit, split=(), kind=jnp.bfloat16):
    drawn = deviation * jax.random.normal(stream_key, dims, jnp.float32)
    if split:
        drawn = drawn * steps_of(stream_key, dims, split, -0.22, 0.18)
    return jnp.clip(drawn, -limit, limit).astype(kind)


def setup_inputs(seed: int = 0) -> dict:
    key_list = jax.random.split(jax.random.key(seed), 4)
    noise_latents = bell_draw(key_list[0], (NR, D), 1.0, 6.0, ((0, 8),))
    data_latents = bell_draw(key_list[1], (NC, D), 1.0, 6.0, ((0, 32),))
    projection = bell_draw(key_list[2], (D, K), D ** -0.5, 0.5)
    return dict(noise_latents=noise_latents, data_latents=data_latents, projection=projection)


epsilon = 0.02


def project_latents(latent_codes, projection):
    return jnp.dot(latent_codes, projection, preferred_element_type=jnp.float32).astype(jnp.bfloat16)


def tile_costs(qrows, rcols, rnorm):
    qnorm = jnp.sum(qrows.astype(jnp.float32) ** 2, axis=1)
    cross = lax.dot_general(qrows, rcols, (((1,), (1,)), ((), ())), preferred_element_type=jnp.float32)
    return (qnorm[:, None] + rnorm[None, :] - 2.0 * cross) / qrows.shape[1]


def reference(noise_latents, data_latents, projection):
    qrows = project_latents(noise_latents, projection)
    rcols = project_latents(data_latents, projection)
    rnorm = jnp.sum(rcols.astype(jnp.float32) ** 2, axis=1)
    block = math.gcd(NR, 512)
    nblocks = NR // block
    qblocks = qrows.reshape(nblocks, block, qrows.shape[1])

    def column_update(frow):
        fblocks = frow.reshape(nblocks, block)

        def step(carry, index):
            top, total = carry
            z_vals = (fblocks[index][:, None] - tile_costs(qblocks[index], rcols, rnorm)) / epsilon
            new_top = jnp.maximum(top, jnp.max(z_vals, axis=0))
            total = total * jnp.exp(top - new_top) + jnp.sum(jnp.exp(z_vals - new_top[None, :]), axis=0)
            return (new_top, total), None

        start = (jnp.full((NC,), -1e30, jnp.float32), jnp.zeros((NC,), jnp.float32))
        (top, total), unused = lax.scan(step, start, jnp.arange(nblocks))
        return -epsilon * (top + jnp.log(total) - math.log(NR))

    def row_block(gcol, qblock):
        z_vals = (gcol[None, :] - tile_costs(qblock, rcols, rnorm)) / epsilon
        top = jnp.max(z_vals, axis=1)
        return top + jnp.log(jnp.sum(jnp.exp(z_vals - top[:, None]), axis=1))

    initial_data_dual = column_update(jnp.zeros((NR,), jnp.float32))
    lse_rows = lax.map(lambda qb: row_block(initial_data_dual, qb), qblocks).reshape(NR)
    f_first = -epsilon * (lse_rows - math.log(NC))
    data_side_potential = column_update(f_first)

    target_groups = data_latents.reshape(N_DP, C_DEV, data_latents.shape[1]).astype(jnp.float32)

    def final_block(qblock):
        z_vals = (data_side_potential[None, :] - tile_costs(qblock, rcols, rnorm)) / epsilon
        z_vals = z_vals.reshape(qblock.shape[0], N_DP, C_DEV)
        block_top = jnp.max(z_vals, axis=2)
        weights = jnp.exp(z_vals - block_top[:, :, None])
        den_parts = jnp.sum(weights, axis=2)
        rounded_values = weights.astype(jnp.bfloat16).astype(jnp.float32)
        partition_count = jnp.einsum('xsm,smw->xsw', rounded_values, target_groups)
        row_top = jnp.max(block_top, axis=1)
        scale = jnp.exp(block_top - row_top[:, None])
        num = jnp.sum(partition_count * scale[:, :, None], axis=1)
        den = jnp.sum(den_parts * scale, axis=1)
        return num / den[:, None]

    targets = lax.map(final_block, qblocks).reshape(NR, data_latents.shape[1])
    return targets, data_side_potential
```

```python
import functools
import math

import jax
import jax.numpy as jnp
from jax import lax
from jax.experimental import pallas as pl
from jax.experimental.pallas import tpu as pltpu
from jax.sharding import PartitionSpec as P

epsilon = 0.02
LOG2E = 1.0 / math.log(2.0)
LN2 = math.log(2.0)
NT = (((1,), (1,)), ((), ()))
MESH = pl.DeviceIdType.MESH
LANES = 128


def ring_sizes(dp):
    return {32: (4, 8), 8: (2, 4), 16: (4, 4)}[dp]


def split3(x):
    hi = x.astype(jnp.bfloat16).astype(jnp.float32)
    rest = x - hi
    mid = rest.astype(jnp.bfloat16).astype(jnp.float32)
    return hi, mid, rest - mid


def kernel(
    cfg,
    noise_ref,
    data_ref,
    proj_ref,
    targets_ref,
    pot_ref,
    q_ref,
    r_ref,
    p_ref,
    d_ref,
    proj2_ref,
    ul_ref,
    vl_ref,
    st1_ref,
    st2_ref,
    rb2_ref,
    f_ref,
    st3_ref,
    num1_ref,
    num2_ref,
    ry1_ref,
    rz1_ref,
    rz2_ref,
    ry2_ref,
    s1_send,
    s1_recv,
    s2_send,
    s2_recv,
    sf_send,
    sf_recv,
    s3_send,
    s3_recv,
    y1_sem,
    z1_sem,
    z2_sem,
    y2_sem,
):
    rows, cols, n_noise, n_dp, kdim = cfg
    ys, zs = ring_sizes(n_dp)
    rch, cch = rows // LANES, cols // LANES
    log_rows = math.log2(rows * n_noise)
    log_cols = math.log2(cols * n_dp)
    scale = 2.0 * LOG2E / (kdim * epsilon)
    norm_scale = LOG2E / (kdim * epsilon)
    me_n = lax.axis_index("noise")
    me_d = lax.axis_index("dp")
    me_y, me_z = me_d // zs, me_d % zs

    barrier = pltpu.get_barrier_semaphore()

    def greet_noise(k, carry):
        pl.semaphore_signal(
            barrier, inc=1, device_id=((me_n + k) % n_noise, me_d), device_id_type=MESH
        )
        return carry

    def greet_dp(k, carry):
        pl.semaphore_signal(
            barrier, inc=1, device_id=(me_n, (me_d + k) % n_dp), device_id_type=MESH
        )
        return carry

    lax.fori_loop(1, n_noise, greet_noise, 0)
    lax.fori_loop(1, n_dp, greet_dp, 0)

    proj2_ref[:, 0:kdim] = proj_ref[...]
    proj2_ref[:, kdim : 2 * kdim] = proj_ref[...]
    half = jnp.full((8, LANES), 0.5, jnp.bfloat16)
    one = jnp.ones((1, LANES), jnp.float32)
    zero = jnp.zeros((2, LANES), jnp.float32)

    def put_bias(dst_ref, c, bias, first):
        parts = list(split3(bias))
        ones = [one, one, one]
        tile = jnp.concatenate((parts + ones if first else ones + parts) + [zero], axis=0)
        dst_ref[c * LANES : (c + 1) * LANES, 128:136] = tile.T.astype(jnp.bfloat16)

    def prepare(src_ref, dst_ref, bias_ref, count, is_q):
        step = min(512, count)

        def body(b, carry):
            sl = pl.ds(pl.multiple_of(b * step, step), step)
            proj = jnp.dot(src_ref[sl, :], proj2_ref[...], preferred_element_type=jnp.float32)
            code = proj.astype(jnp.bfloat16)
            full = code.astype(jnp.float32)
            square = full * full
            sq_hi = square.astype(jnp.bfloat16)
            sq_lo = (square - sq_hi.astype(jnp.float32)).astype(jnp.bfloat16)
            norm = lax.dot_general(
                half, sq_hi, NT, preferred_element_type=jnp.float32
            ) + lax.dot_general(half, sq_lo, NT, preferred_element_type=jnp.float32)
            if is_q:
                dst_ref[sl, 0:128] = code
            else:
                scaled = full * scale
                hi = scaled.astype(jnp.bfloat16)
                lo = (scaled - hi.astype(jnp.float32)).astype(jnp.bfloat16)
                lane = lax.broadcasted_iota(jnp.int32, scaled.shape, 1)
                dst_ref[sl, 0:128] = jnp.where(
                    lane < kdim, hi.astype(jnp.float32), lo.astype(jnp.float32)
                ).astype(jnp.bfloat16)
            dst_ref[sl, 128:256] = jnp.zeros((step, 128), jnp.bfloat16)
            for c in range(step // LANES):
                bias_ref[pl.ds(b * (step // LANES) + c, 1), :] = (
                    -norm_scale * norm[0:1, c * LANES : (c + 1) * LANES]
                )
            return carry

        lax.fori_loop(0, count // step, body, 0)
        bias = bias_ref[...]
        for c in range(count // LANES):
            put_bias(dst_ref, c, bias[c : c + 1, :], is_q)

    prepare(noise_ref, q_ref, ul_ref, rows, True)
    prepare(data_ref, r_ref, vl_ref, cols, False)

    def lse_pass(lhs_ref, count, rhs_ref, width, write):
        bw = min(2048, width)
        bl = 256
        un = 2

        def wide(w, carry):
            rhs = rhs_ref[pl.ds(pl.multiple_of(w * bw, bw), bw), :]

            def body(step, state):
                top, total = state
                for u in range(un):
                    sl = pl.ds(pl.multiple_of((step * un + u) * bl, bl), bl)
                    z = lax.dot_general(
                        lhs_ref[sl, :], rhs, NT, preferred_element_type=jnp.float32
                    ).reshape(bl // 8, 8, bw)
                    new = jnp.maximum(top, jnp.max(z, axis=0))
                    total = total * jnp.exp2(top - new) + jnp.sum(jnp.exp2(z - new[None]), axis=0)
                    top = new
                return top, total

            start = (jnp.full((8, bw), -1e30, jnp.float32), jnp.zeros((8, bw), jnp.float32))
            top, total = lax.fori_loop(0, count // (bl * un), body, start)
            best = jnp.max(top, axis=0, keepdims=True)
            write(w, bw, best, jnp.sum(total * jnp.exp2(top - best), axis=0, keepdims=True))
            return carry

        lax.fori_loop(0, width // bw, wide, 0)

    def write1(w, bw, top, total):
        for c in range(bw // LANES):
            lanes = slice(c * LANES, (c + 1) * LANES)
            st1_ref[me_n, 0, pl.ds(w * (bw // LANES) + c, 1), :] = top[:, lanes]
            st1_ref[me_n, 1, pl.ds(w * (bw // LANES) + c, 1), :] = total[:, lanes]

    def write2(w, bw, top, total):
        for c in range(bw // LANES):
            lanes = slice(c * LANES, (c + 1) * LANES)
            st2_ref[w * (bw // LANES) + c, 0:1, :] = top[:, lanes]
            st2_ref[w * (bw // LANES) + c, 1:2, :] = total[:, lanes]

    lse_pass(q_ref, rows, r_ref, cols, write1)
    pl.semaphore_wait(barrier, n_noise - 1 + n_dp - 1)

    def gather_noise(ref, send_sem, recv_sem):
        def copy(k):
            return pltpu.make_async_remote_copy(
                src_ref=ref.at[me_n],
                dst_ref=ref.at[me_n],
                send_sem=send_sem.at[k],
                recv_sem=recv_sem.at[me_n],
                device_id=((me_n + k) % n_noise, me_d),
                device_id_type=MESH,
            )

        def start(k, carry):
            copy(k).start()
            return carry

        def wait(k, carry):
            source = (me_n + n_noise - k) % n_noise
            pltpu.make_async_copy(ref.at[source], ref.at[source], recv_sem.at[source]).wait()
            copy(k).wait_send()
            return carry

        lax.fori_loop(1, n_noise, start, 0)
        lax.fori_loop(1, n_noise, wait, 0)

    gather_noise(st1_ref, s1_send, s1_recv)
    top = st1_ref[0, 0]
    for k in range(1, n_noise):
        top = jnp.maximum(top, st1_ref[k, 0])
    total = st1_ref[0, 1] * jnp.exp2(st1_ref[0, 0] - top)
    for k in range(1, n_noise):
        total = total + st1_ref[k, 1] * jnp.exp2(st1_ref[k, 0] - top)
    g1 = log_rows - (top + jnp.log(total) * LOG2E)
    vl = vl_ref[...] + g1
    for c in range(cch):
        put_bias(r_ref, c, vl[c : c + 1, :], False)

    lse_pass(r_ref, cols, q_ref, rows, write2)

    def scatter(k):
        other = (me_d + k) % n_dp
        return pltpu.make_async_remote_copy(
            src_ref=st2_ref.at[other],
            dst_ref=rb2_ref.at[me_d],
            send_sem=s2_send.at[k],
            recv_sem=s2_recv.at[me_d],
            device_id=(me_n, other),
            device_id_type=MESH,
        )

    def back(k):
        return pltpu.make_async_remote_copy(
            src_ref=f_ref.at[me_d],
            dst_ref=f_ref.at[me_d],
            send_sem=sf_send.at[k],
            recv_sem=sf_recv.at[me_d],
            device_id=(me_n, (me_d + k) % n_dp),
            device_id_type=MESH,
        )

    def start_scatter(k, carry):
        scatter(k).start()
        return carry

    def wait_scatter(k, carry):
        source = (me_d + n_dp - k) % n_dp
        pltpu.make_async_copy(rb2_ref.at[source], rb2_ref.at[source], s2_recv.at[source]).wait()
        scatter(k).wait_send()
        return carry

    def start_back(k, carry):
        back(k).start()
        return carry

    def wait_back(k, carry):
        source = (me_d + n_dp - k) % n_dp
        pltpu.make_async_copy(f_ref.at[source], f_ref.at[source], sf_recv.at[source]).wait()
        back(k).wait_send()
        return carry

    lax.fori_loop(1, n_dp, start_scatter, 0)
    rb2_ref[me_d] = st2_ref[me_d]
    lax.fori_loop(1, n_dp, wait_scatter, 0)
    tops = rb2_ref[:, 0, :]
    sums = rb2_ref[:, 1, :]
    top = jnp.max(tops, axis=0, keepdims=True)
    total = jnp.sum(sums * jnp.exp2(tops - top), axis=0, keepdims=True)
    f_ref[me_d] = log_cols - (top + jnp.log(total) * LOG2E)
    lax.fori_loop(1, n_dp, start_back, 0)
    lax.fori_loop(1, n_dp, wait_back, 0)
    ul = ul_ref[...]
    for c in range(rch):
        put_bias(q_ref, c, ul[c : c + 1, :] + f_ref[c], True)

    bl, bw, un = 256, cols, 2

    def plan(step, total):
        for u in range(un):
            sl = pl.ds(pl.multiple_of((step * un + u) * bl, bl), bl)
            z = lax.dot_general(q_ref[sl, :], r_ref[...], NT, preferred_element_type=jnp.float32)
            p = jnp.exp2(z)
            p_ref[sl, :] = p.astype(jnp.bfloat16)
            total = total + jnp.sum(p.reshape(bl // 8, 8, bw), axis=0)
        return total

    total = lax.fori_loop(0, rows // (bl * un), plan, jnp.zeros((8, bw), jnp.float32))
    total = jnp.sum(total, axis=0, keepdims=True)
    for c in range(cch):
        st3_ref[me_n, c : c + 1, :] = total[:, c * LANES : (c + 1) * LANES]
    gather_noise(st3_ref, s3_send, s3_recv)
    total = st3_ref[0]
    for k in range(1, n_noise):
        total = total + st3_ref[k]
    pot_ref[...] = (epsilon * LN2) * (g1 + log_rows - jnp.log(total) * LOG2E)

    factor = float(rows * n_noise) / total
    f_hi = factor.astype(jnp.bfloat16).astype(jnp.float32)
    f_lo = factor - f_hi
    zero5 = jnp.zeros((5, LANES), jnp.float32)
    for c in range(cch):
        sl = slice(c * LANES, (c + 1) * LANES)
        tile = jnp.concatenate(
            [f_hi[c : c + 1], f_lo[c : c + 1], factor[c : c + 1], zero5], axis=0
        ).T
        d_ref[sl, 0:128] = (data_ref[sl, :].astype(jnp.float32) * tile[:, 2:3]).astype(
            jnp.bfloat16
        )
        d_ref[sl, 128:256] = jnp.zeros((LANES, 128), jnp.bfloat16)
        d_ref[sl, 128:136] = tile.astype(jnp.bfloat16)

    def weigh(y, carry):
        n = zs * LANES
        sl = pl.ds(pl.multiple_of(y * n, n), n)
        both = jnp.dot(p_ref[sl, :], d_ref[...], preferred_element_type=jnp.float32)
        for z in range(zs):
            part = both[z * LANES : (z + 1) * LANES]
            num1_ref[y, z, 0:64, :] = part[0:64, 0:128]
            num1_ref[y, z, 64:72, :] = part[:, 128:136].T
            num2_ref[z, y, :, :] = part[64:128, 0:128]
        return carry

    lax.fori_loop(0, ys, weigh, 0)

    def ring(block, recv_ref, sem, size, me, peer, cut):
        h = size // 2
        right, left = peer((me + 1) % size), peer((me + size - 1) % size)

        def copies(k):
            ahead, behind = (me + k) % size, (me + size - k) % size
            first = block(ahead, slice(0, cut)) if k == h else block(ahead, None)
            second = block(behind, slice(cut, None)) if k == h else block(behind, None)
            land = [recv_ref.at[2 * (k - 1)], recv_ref.at[2 * (k - 1) + 1]]
            if k == h:
                land = [land[0].at[0:cut], land[1].at[cut : recv_ref.shape[1]]]
            out = []
            for i, (src, dst, dev) in enumerate(((first, land[0], right), (second, land[1], left))):
                out.append(
                    pltpu.make_async_remote_copy(
                        src_ref=src,
                        dst_ref=dst,
                        send_sem=sem.at[0, k - 1, i],
                        recv_sem=sem.at[1, k - 1, i],
                        device_id=dev,
                        device_id_type=MESH,
                    )
                )
            return out

        def add(k):
            for i, target in enumerate(((me + k - 1) % size, (me + size - k + 1) % size)):
                sl = None
                if k == h:
                    sl = slice(0, cut) if i == 0 else slice(cut, recv_ref.shape[1])
                dst = block(target, sl)
                src = recv_ref.at[2 * (k - 1) + i]
                if sl is not None:
                    src = src.at[sl]
                dst[...] = dst[...] + src[...]

        return copies, add, h

    def peer_y(y):
        return (me_n, y * zs + me_z)

    def peer_z(z):
        return (me_n, me_y * zs + z)

    def cutter(ref, extent):
        def block(index, sl):
            if sl is None:
                return ref.at[index]
            return ref.at[index, sl.start : (extent if sl.stop is None else sl.stop)]

        return block

    def run(stages):
        most = max(h for _, _, h in stages)
        for k in range(most, 0, -1):
            live = [(copies(k), add) for copies, add, h in stages if k <= h]
            for pair, _ in live:
                for c in pair:
                    c.start()
            for pair, add in live:
                for c in pair:
                    c.wait()
                add(k)

    run(
        [
            ring(cutter(num1_ref, zs), ry1_ref, y1_sem, ys, me_y, peer_y, zs // 2),
            ring(cutter(num2_ref, ys), rz2_ref, z2_sem, zs, me_z, peer_z, ys // 2),
        ]
    )
    run(
        [
            ring(cutter(num1_ref.at[me_y], 72), rz1_ref, z1_sem, zs, me_z, peer_z, 40),
            ring(cutter(num2_ref.at[me_z], 64), ry2_ref, y2_sem, ys, me_y, peer_y, 32),
        ]
    )
    mine = num1_ref[me_y, me_z]
    den = (mine[64:72]).T
    den = den[:, 0:1] + den[:, 1:2]
    targets_ref[0:64, :] = mine[0:64] / den[0:64]
    targets_ref[64:128, :] = num2_ref[me_z, me_y] / den[64:128]


def shards(noise_latents, data_latents, projection):
    rows, width = noise_latents.shape
    cols = data_latents.shape[0]
    kdim = projection.shape[1]
    n_noise, n_dp = lax.axis_size("noise"), lax.axis_size("dp")
    ys, zs = ring_sizes(n_dp)
    rch, cch = rows // LANES, cols // LANES
    f32, bf16 = jnp.float32, jnp.bfloat16
    cfg = (rows, cols, n_noise, n_dp, kdim)
    dma = pltpu.SemaphoreType.DMA
    vmem = pl.BlockSpec(memory_space=pltpu.VMEM)
    targets, pot = pl.pallas_call(
        functools.partial(kernel, cfg),
        out_shape=(
            jax.ShapeDtypeStruct((LANES, width), f32),
            jax.ShapeDtypeStruct((cch, LANES), f32),
        ),
        in_specs=[vmem] * 3,
        out_specs=(vmem, vmem),
        scratch_shapes=[
            pltpu.VMEM((rows, 256), bf16),
            pltpu.VMEM((cols, 256), bf16),
            pltpu.VMEM((rows, cols), bf16),
            pltpu.VMEM((cols, 256), bf16),
            pltpu.VMEM((width, 2 * kdim), bf16),
            pltpu.VMEM((rch, LANES), f32),
            pltpu.VMEM((cch, LANES), f32),
            pltpu.VMEM((n_noise, 2, cch, LANES), f32),
            pltpu.VMEM((n_dp, 2, LANES), f32),
            pltpu.VMEM((n_dp, 2, LANES), f32),
            pltpu.VMEM((n_dp, 1, LANES), f32),
            pltpu.VMEM((n_noise, cch, LANES), f32),
            pltpu.VMEM((ys, zs, 72, LANES), f32),
            pltpu.VMEM((zs, ys, 64, LANES), f32),
            pltpu.VMEM((ys, zs, 72, LANES), f32),
            pltpu.VMEM((zs, 72, LANES), f32),
            pltpu.VMEM((zs, ys, 64, LANES), f32),
            pltpu.VMEM((ys, 64, LANES), f32),
            dma((n_noise,)),
            dma((n_noise,)),
            dma((n_dp,)),
            dma((n_dp,)),
            dma((n_dp,)),
            dma((n_dp,)),
            dma((n_noise,)),
            dma((n_noise,)),
            dma((2, ys // 2, 2)),
            dma((2, zs // 2, 2)),
            dma((2, zs // 2, 2)),
            dma((2, ys // 2, 2)),
        ],
        compiler_params=pltpu.CompilerParams(
            collective_id=0, has_side_effects=True, vmem_limit_bytes=56 * 2**20
        ),
        cost_estimate=pl.CostEstimate(
            flops=8 * rows * cols * 256, bytes_accessed=2**21, transcendentals=3 * rows * cols
        ),
    )(noise_latents, data_latents, projection)
    return (targets, pot.reshape(cols))


def solution(mesh):
    in_specs = (P("noise", None), P("dp", None), P())
    out_specs = (P(("noise", "dp"), None), P("dp"))
    return jax.shard_map(shards, mesh=mesh, in_specs=in_specs, out_specs=out_specs, check_vma=False)
```

```python
import functools
import math

import jax
import jax.numpy as jnp
from jax import lax
from jax.experimental import pallas as pl
from jax.experimental.pallas import tpu as pltpu
from jax.sharding import PartitionSpec as P

epsilon = 0.02
LOG2E = 1.0 / math.log(2.0)
LN2 = math.log(2.0)
NT = (((1,), (1,)), ((), ()))
MESH = pl.DeviceIdType.MESH
LANES = 128


def ring_sizes(dp):
    return {32: (4, 8), 8: (2, 4), 16: (4, 4)}[dp]


def split3(x):
    hi = x.astype(jnp.bfloat16).astype(jnp.float32)
    rest = x - hi
    mid = rest.astype(jnp.bfloat16).astype(jnp.float32)
    return hi, mid, rest - mid


def kernel(
    cfg,
    noise_ref,
    data_ref,
    proj_ref,
    targets_ref,
    pot_ref,
    q_ref,
    r_ref,
    p_ref,
    d_ref,
    proj2_ref,
    ul_ref,
    vl_ref,
    st1_ref,
    st2_ref,
    rb2_ref,
    f_ref,
    st3_ref,
    num1_ref,
    num2_ref,
    ry1_ref,
    rz1_ref,
    rz2_ref,
    ry2_ref,
    s1_send,
    s1_recv,
    s2_send,
    s2_recv,
    sf_send,
    sf_recv,
    s3_send,
    s3_recv,
    y1_sem,
    z1_sem,
    z2_sem,
    y2_sem,
):
    rows, cols, n_noise, n_dp, kdim = cfg
    ys, zs = ring_sizes(n_dp)
    rch, cch = rows // LANES, cols // LANES
    log_rows = math.log2(rows * n_noise)
    log_cols = math.log2(cols * n_dp)
    scale = 2.0 * LOG2E / (kdim * epsilon)
    norm_scale = LOG2E / (kdim * epsilon)
    me_n = lax.axis_index("noise")
    me_d = lax.axis_index("dp")
    me_y, me_z = me_d // zs, me_d % zs

    barrier = pltpu.get_barrier_semaphore()

    def greet_noise(k, carry):
        pl.semaphore_signal(
            barrier, inc=1, device_id=((me_n + k) % n_noise, me_d), device_id_type=MESH
        )
        return carry

    def greet_dp(k, carry):
        pl.semaphore_signal(
            barrier, inc=1, device_id=(me_n, (me_d + k) % n_dp), device_id_type=MESH
        )
        return carry

    lax.fori_loop(1, n_noise, greet_noise, 0)
    lax.fori_loop(1, n_dp, greet_dp, 0)

    proj2_ref[0:kdim, :] = proj_ref[...]
    proj2_ref[kdim : 2 * kdim, :] = proj_ref[...]
    half = jnp.full((8, LANES), 0.5, jnp.bfloat16)
    one = jnp.ones((1, LANES), jnp.float32)
    zero = jnp.zeros((2, LANES), jnp.float32)

    def put_bias(dst_ref, c, bias, first):
        parts = list(split3(bias))
        ones = [one, one, one]
        tile = jnp.concatenate((parts + ones if first else ones + parts) + [zero], axis=0)
        dst_ref[c * LANES : (c + 1) * LANES, 128:136] = tile.T.astype(jnp.bfloat16)

    def prepare(src_ref, dst_ref, bias_ref, count, is_q):
        step = min(512, count)

        def body(b, carry):
            sl = pl.ds(pl.multiple_of(b * step, step), step)
            proj = lax.dot_general(
                src_ref[sl, :], proj2_ref[...], NT, preferred_element_type=jnp.float32
            )
            code = proj.astype(jnp.bfloat16)
            full = code.astype(jnp.float32)
            square = full * full
            sq_hi = square.astype(jnp.bfloat16)
            sq_lo = (square - sq_hi.astype(jnp.float32)).astype(jnp.bfloat16)
            norm = lax.dot_general(
                half, sq_hi, NT, preferred_element_type=jnp.float32
            ) + lax.dot_general(half, sq_lo, NT, preferred_element_type=jnp.float32)
            if is_q:
                dst_ref[sl, 0:128] = code
            else:
                scaled = full * scale
                hi = scaled.astype(jnp.bfloat16)
                lo = (scaled - hi.astype(jnp.float32)).astype(jnp.bfloat16)
                lane = lax.broadcasted_iota(jnp.int32, scaled.shape, 1)
                dst_ref[sl, 0:128] = jnp.where(
                    lane < kdim, hi.astype(jnp.float32), lo.astype(jnp.float32)
                ).astype(jnp.bfloat16)
            dst_ref[sl, 128:256] = jnp.zeros((step, 128), jnp.bfloat16)
            for c in range(step // LANES):
                bias_ref[pl.ds(b * (step // LANES) + c, 1), :] = (
                    -norm_scale * norm[0:1, c * LANES : (c + 1) * LANES]
                )
            return carry

        lax.fori_loop(0, count // step, body, 0)
        bias = bias_ref[...]
        for c in range(count // LANES):
            put_bias(dst_ref, c, bias[c : c + 1, :], is_q)

    prepare(noise_ref, q_ref, ul_ref, rows, True)
    prepare(data_ref, r_ref, vl_ref, cols, False)

    def lse_pass(lhs_ref, count, rhs_ref, width, write):
        bw = min(2048, width)
        bl = 256
        un = min(4, count // bl)

        def wide(w, carry):
            rhs = rhs_ref[pl.ds(pl.multiple_of(w * bw, bw), bw), :]

            def body(step, state):
                top, total = state
                for u in range(un):
                    sl = pl.ds(pl.multiple_of((step * un + u) * bl, bl), bl)
                    z = lax.dot_general(
                        lhs_ref[sl, :], rhs, NT, preferred_element_type=jnp.float32
                    ).reshape(bl // 8, 8, bw)
                    new = jnp.maximum(top, jnp.max(z, axis=0))
                    total = total * jnp.exp2(top - new) + jnp.sum(jnp.exp2(z - new[None]), axis=0)
                    top = new
                return top, total

            start = (jnp.full((8, bw), -1e30, jnp.float32), jnp.zeros((8, bw), jnp.float32))
            top, total = lax.fori_loop(0, count // (bl * un), body, start)
            best = jnp.max(top, axis=0, keepdims=True)
            write(w, bw, best, jnp.sum(total * jnp.exp2(top - best), axis=0, keepdims=True))
            return carry

        lax.fori_loop(0, width // bw, wide, 0)

    def write1(w, bw, top, total):
        for c in range(bw // LANES):
            lanes = slice(c * LANES, (c + 1) * LANES)
            st1_ref[me_n, 0, pl.ds(w * (bw // LANES) + c, 1), :] = top[:, lanes]
            st1_ref[me_n, 1, pl.ds(w * (bw // LANES) + c, 1), :] = total[:, lanes]

    def write2(w, bw, top, total):
        for c in range(bw // LANES):
            lanes = slice(c * LANES, (c + 1) * LANES)
            st2_ref[w * (bw // LANES) + c, 0:1, :] = top[:, lanes]
            st2_ref[w * (bw // LANES) + c, 1:2, :] = total[:, lanes]

    lse_pass(q_ref, rows, r_ref, cols, write1)
    pl.semaphore_wait(barrier, n_noise - 1 + n_dp - 1)

    def gather_noise(ref, send_sem, recv_sem):
        def copy(k):
            return pltpu.make_async_remote_copy(
                src_ref=ref.at[me_n],
                dst_ref=ref.at[me_n],
                send_sem=send_sem.at[k],
                recv_sem=recv_sem.at[me_n],
                device_id=((me_n + k) % n_noise, me_d),
                device_id_type=MESH,
            )

        def start(k, carry):
            copy(k).start()
            return carry

        def wait(k, carry):
            source = (me_n + n_noise - k) % n_noise
            pltpu.make_async_copy(ref.at[source], ref.at[source], recv_sem.at[source]).wait()
            copy(k).wait_send()
            return carry

        lax.fori_loop(1, n_noise, start, 0)
        lax.fori_loop(1, n_noise, wait, 0)

    gather_noise(st1_ref, s1_send, s1_recv)
    top = st1_ref[0, 0]
    for k in range(1, n_noise):
        top = jnp.maximum(top, st1_ref[k, 0])
    total = st1_ref[0, 1] * jnp.exp2(st1_ref[0, 0] - top)
    for k in range(1, n_noise):
        total = total + st1_ref[k, 1] * jnp.exp2(st1_ref[k, 0] - top)
    g1 = log_rows - (top + jnp.log(total) * LOG2E)
    vl = vl_ref[...] + g1
    for c in range(cch):
        put_bias(r_ref, c, vl[c : c + 1, :], False)

    lse_pass(r_ref, cols, q_ref, rows, write2)

    def scatter(k):
        other = (me_d + k) % n_dp
        return pltpu.make_async_remote_copy(
            src_ref=st2_ref.at[other],
            dst_ref=rb2_ref.at[me_d],
            send_sem=s2_send.at[k],
            recv_sem=s2_recv.at[me_d],
            device_id=(me_n, other),
            device_id_type=MESH,
        )

    def back(k):
        return pltpu.make_async_remote_copy(
            src_ref=f_ref.at[me_d],
            dst_ref=f_ref.at[me_d],
            send_sem=sf_send.at[k],
            recv_sem=sf_recv.at[me_d],
            device_id=(me_n, (me_d + k) % n_dp),
            device_id_type=MESH,
        )

    def start_scatter(k, carry):
        scatter(k).start()
        return carry

    def wait_scatter(k, carry):
        source = (me_d + n_dp - k) % n_dp
        pltpu.make_async_copy(rb2_ref.at[source], rb2_ref.at[source], s2_recv.at[source]).wait()
        scatter(k).wait_send()
        return carry

    def start_back(k, carry):
        back(k).start()
        return carry

    def wait_back(k, carry):
        source = (me_d + n_dp - k) % n_dp
        pltpu.make_async_copy(f_ref.at[source], f_ref.at[source], sf_recv.at[source]).wait()
        back(k).wait_send()
        return carry

    lax.fori_loop(1, n_dp, start_scatter, 0)
    rb2_ref[me_d] = st2_ref[me_d]
    lax.fori_loop(1, n_dp, wait_scatter, 0)
    tops = rb2_ref[:, 0, :]
    sums = rb2_ref[:, 1, :]
    top = jnp.max(tops, axis=0, keepdims=True)
    total = jnp.sum(sums * jnp.exp2(tops - top), axis=0, keepdims=True)
    f_ref[me_d] = log_cols - (top + jnp.log(total) * LOG2E)
    lax.fori_loop(1, n_dp, start_back, 0)
    lax.fori_loop(1, n_dp, wait_back, 0)
    ul = ul_ref[...]
    for c in range(rch):
        put_bias(q_ref, c, ul[c : c + 1, :] + f_ref[c], True)

    bl, bw, un = 256, cols, min(4, rows // 256)
    per = bl // LANES

    def plan(step, total):
        for u in range(un):
            tile = step * un + u
            sl = pl.ds(pl.multiple_of(tile * bl, bl), bl)
            z = lax.dot_general(q_ref[sl, :], r_ref[...], NT, preferred_element_type=jnp.float32)
            p = jnp.exp2(z)
            half_p = p.astype(jnp.bfloat16)
            for i in range(per):
                chunk = tile * per + i
                put = pl.ds(pl.multiple_of(chunk // zs * LANES, LANES), LANES)
                p_ref[chunk % zs, put, :] = half_p[i * LANES : (i + 1) * LANES]
            total = total + jnp.sum(p.reshape(bl // 8, 8, bw), axis=0)
        return total

    total = lax.fori_loop(0, rows // (bl * un), plan, jnp.zeros((8, bw), jnp.float32))
    total = jnp.sum(total, axis=0, keepdims=True)
    for c in range(cch):
        st3_ref[me_n, c : c + 1, :] = total[:, c * LANES : (c + 1) * LANES]
    gather_noise(st3_ref, s3_send, s3_recv)
    total = st3_ref[0]
    for k in range(1, n_noise):
        total = total + st3_ref[k]
    pot_ref[...] = (epsilon * LN2) * (g1 + log_rows - jnp.log(total) * LOG2E)

    factor = float(rows * n_noise) / total
    f_hi = factor.astype(jnp.bfloat16).astype(jnp.float32)
    f_lo = factor - f_hi
    zero5 = jnp.zeros((5, LANES), jnp.float32)
    for c in range(cch):
        sl = slice(c * LANES, (c + 1) * LANES)
        tile = jnp.concatenate(
            [f_hi[c : c + 1], f_lo[c : c + 1], factor[c : c + 1], zero5], axis=0
        ).T
        d_ref[sl, 0:128] = (data_ref[sl, :].astype(jnp.float32) * tile[:, 2:3]).astype(
            jnp.bfloat16
        )
        d_ref[sl, 128:256] = jnp.zeros((LANES, 128), jnp.bfloat16)
        d_ref[sl, 128:136] = tile.astype(jnp.bfloat16)

    h = zs // 2
    offsets = [h]
    for k in range(h - 1, 0, -1):
        offsets += [k, zs - k]
    offsets.append(0)
    y_steps = [2, 1, 3] if ys == 4 else [1]
    pending = []

    def peer_y(step):
        return (me_n, (me_y + step) % ys * zs + me_z)

    def peer_z(step):
        return (me_n, me_y * zs + (me_z + step) % zs)

    def send(src, dst, sends, recvs, device):
        copy = pltpu.make_async_remote_copy(
            src_ref=src,
            dst_ref=dst,
            send_sem=sends,
            recv_sem=recvs,
            device_id=device,
            device_id_type=MESH,
        )
        copy.start()
        pending.append(copy)

    def arrived(ref, sem):
        pltpu.make_async_copy(ref, ref, sem).wait()

    def weigh(off):
        zt = (me_z + off) % zs
        both = jnp.dot(p_ref[zt], d_ref[...], preferred_element_type=jnp.float32)
        for y in range(ys):
            part = both[y * LANES : (y + 1) * LANES]
            num1_ref[zt, y, 0:64, :] = part[0:64, 0:128]
            num1_ref[zt, y, 64:72, :] = part[:, 128:136].T
            num2_ref[zt, y, :, :] = part[64:128, 0:128]

    def y_first(off):
        i = offsets.index(off)
        zt = (me_z + off) % zs
        for step in y_steps:
            send(
                num1_ref.at[zt, (me_y + step) % ys],
                ry1_ref.at[step - 1, i],
                y1_sem.at[0, step - 1, i],
                y1_sem.at[1, step - 1, i],
                peer_y(step),
            )

    def y_merge(off):
        i = offsets.index(off)
        zt = (me_z + off) % zs
        for step in y_steps:
            arrived(ry1_ref.at[step - 1, i], y1_sem.at[1, step - 1, i])
        total = num1_ref[zt, me_y]
        for step in range(1, ys):
            total = total + ry1_ref[step - 1, i]
        num1_ref[zt, me_y] = total
        if off:
            send(num1_ref.at[zt, me_y], rz1_ref.at[i], z1_sem.at[0, i], z1_sem.at[1, i], peer_z(off))

    def z_send(k, way, chunks):
        zt = (me_z + (k if way == 0 else zs - k)) % zs
        for y in chunks:
            send(
                num2_ref.at[zt, y],
                rz2_ref.at[way, k - 1, y],
                z2_sem.at[0, way, k - 1, y],
                z2_sem.at[1, way, k - 1, y],
                peer_z(1 if way == 0 else zs - 1),
            )

    def z_merge(k, way, chunks):
        zt = (me_z + (k if way == 0 else zs - k)) % zs
        for y in chunks:
            arrived(rz2_ref.at[way, k, y], z2_sem.at[1, way, k, y])
            num2_ref[zt, y] = num2_ref[zt, y] + rz2_ref[way, k, y]

    every = list(range(ys))
    parts = [every[: ys // 2], every[ys // 2 :]]

    def z_step(k, merged):
        for way in range(2):
            z_merge(k, way, merged[way])
            z_send(k, way, merged[way])

    weigh(h)
    z_send(h, 0, parts[0])
    z_send(h, 1, parts[1])
    y_first(h)
    queue = offsets[1:]
    for _ in range(min(2, len(queue) - 1)):
        off = queue.pop(0)
        weigh(off)
        if h > 1:
            z_send(h - 1, 0 if off == h - 1 else 1, parts[1] if off == h - 1 else parts[0])
        y_first(off)
    for n, off in enumerate(queue):
        weigh(off)
        y_first(off)
        if n == 2 and h > 1:
            z_step(h - 1, parts)
    if len(queue) < 3 and h > 1:
        z_step(h - 1, parts)
    waiting = list(offsets)
    for k in range(h - 2, 0, -1):
        for _ in range(2):
            y_merge(waiting.pop(0))
        z_step(k, [every, every])
    while len(waiting) > 2:
        y_merge(waiting.pop(0))
    if h > 0:
        z_merge(0, 0, every if h > 1 else parts[0])
        z_merge(0, 1, every if h > 1 else parts[1])
    for step in y_steps:
        send(
            num2_ref.at[me_z, (me_y + step) % ys],
            ry2_ref.at[step - 1],
            y2_sem.at[0, step - 1],
            y2_sem.at[1, step - 1],
            peer_y(step),
        )
    while waiting:
        y_merge(waiting.pop(0))
    mine = num1_ref[me_z, me_y]
    for i in range(zs - 1):
        arrived(rz1_ref.at[i], z1_sem.at[1, i])
        mine = mine + rz1_ref[i]
    den = (mine[64:72]).T
    den = den[:, 0:1] + den[:, 1:2]
    targets_ref[0:64, :] = mine[0:64] / den[0:64]
    rest = num2_ref[me_z, me_y]
    for step in y_steps:
        arrived(ry2_ref.at[step - 1], y2_sem.at[1, step - 1])
    for step in range(1, ys):
        rest = rest + ry2_ref[step - 1]
    targets_ref[64:128, :] = rest / den[64:128]
    for copy in pending:
        copy.wait_send()


def shards(noise_latents, data_latents, projection):
    rows, width = noise_latents.shape
    cols = data_latents.shape[0]
    kdim = projection.shape[1]
    n_noise, n_dp = lax.axis_size("noise"), lax.axis_size("dp")
    ys, zs = ring_sizes(n_dp)
    rch, cch = rows // LANES, cols // LANES
    f32, bf16 = jnp.float32, jnp.bfloat16
    cfg = (rows, cols, n_noise, n_dp, kdim)
    dma = pltpu.SemaphoreType.DMA
    vmem = pl.BlockSpec(memory_space=pltpu.VMEM)
    targets, pot = pl.pallas_call(
        functools.partial(kernel, cfg),
        out_shape=(
            jax.ShapeDtypeStruct((LANES, width), f32),
            jax.ShapeDtypeStruct((cch, LANES), f32),
        ),
        in_specs=[vmem] * 3,
        out_specs=(vmem, vmem),
        scratch_shapes=[
            pltpu.VMEM((rows, 256), bf16),
            pltpu.VMEM((cols, 256), bf16),
            pltpu.VMEM((zs, ys * LANES, cols), bf16),
            pltpu.VMEM((cols, 256), bf16),
            pltpu.VMEM((2 * kdim, width), bf16),
            pltpu.VMEM((rch, LANES), f32),
            pltpu.VMEM((cch, LANES), f32),
            pltpu.VMEM((n_noise, 2, cch, LANES), f32),
            pltpu.VMEM((n_dp, 2, LANES), f32),
            pltpu.VMEM((n_dp, 2, LANES), f32),
            pltpu.VMEM((n_dp, 1, LANES), f32),
            pltpu.VMEM((n_noise, cch, LANES), f32),
            pltpu.VMEM((zs, ys, 72, LANES), f32),
            pltpu.VMEM((zs, ys, 64, LANES), f32),
            pltpu.VMEM((ys - 1, zs, 72, LANES), f32),
            pltpu.VMEM((zs - 1, 72, LANES), f32),
            pltpu.VMEM((2, zs // 2, ys, 64, LANES), f32),
            pltpu.VMEM((ys - 1, 64, LANES), f32),
            dma((n_noise,)),
            dma((n_noise,)),
            dma((n_dp,)),
            dma((n_dp,)),
            dma((n_dp,)),
            dma((n_dp,)),
            dma((n_noise,)),
            dma((n_noise,)),
            dma((2, ys - 1, zs)),
            dma((2, zs - 1)),
            dma((2, 2, zs // 2, ys)),
            dma((2, ys - 1)),
        ],
        compiler_params=pltpu.CompilerParams(
            collective_id=0, has_side_effects=True, vmem_limit_bytes=56 * 2**20
        ),
        cost_estimate=pl.CostEstimate(
            flops=8 * rows * cols * 256, bytes_accessed=2**21, transcendentals=3 * rows * cols
        ),
    )(noise_latents, data_latents, projection.T)
    return (targets, pot.reshape(cols))


def solution(mesh):
    in_specs = (P("noise", None), P("dp", None), P())
    out_specs = (P(("noise", "dp"), None), P("dp"))
    return jax.shard_map(shards, mesh=mesh, in_specs=in_specs, out_specs=out_specs, check_vma=False)
```

```python
import functools
import math

import jax
import jax.numpy as jnp
from jax import lax
from jax.experimental import pallas as pl
from jax.experimental.pallas import tpu as pltpu
from jax.sharding import PartitionSpec as P

epsilon = 0.02
LOG2E = 1.0 / math.log(2.0)
LN2 = math.log(2.0)
NT = (((1,), (1,)), ((), ()))
MESH = pl.DeviceIdType.MESH
LANES = 128


def ring_sizes(dp):
    return {32: (4, 8), 8: (2, 4), 16: (4, 4)}[dp]


def split3(x):
    hi = x.astype(jnp.bfloat16).astype(jnp.float32)
    rest = x - hi
    mid = rest.astype(jnp.bfloat16).astype(jnp.float32)
    return hi, mid, rest - mid


def kernel(
    cfg,
    noise_ref,
    data_ref,
    proj_ref,
    targets_ref,
    pot_ref,
    q_ref,
    r_ref,
    p_ref,
    d_ref,
    proj2_ref,
    ul_ref,
    vl_ref,
    st1_ref,
    lse_ref,
    rho_ref,
    gy1_ref,
    gz1_ref,
    gz2_ref,
    gy2_ref,
    st3_ref,
    num_ref,
    far_ref,
    near_ref,
    rz_ref,
    s1_sem,
    s3_sem,
    gy1_sem,
    gz1_sem,
    gz2_sem,
    gy2_sem,
    far_sem,
    near_sem,
    rz_sem,
):
    rows, cols, n_noise, n_dp, kdim = cfg
    ys, zs = ring_sizes(n_dp)
    rch, cch = rows // LANES, cols // LANES
    log_rows = math.log2(rows * n_noise)
    log_cols = math.log2(cols * n_dp)
    scale = 2.0 * LOG2E / (kdim * epsilon)
    norm_scale = LOG2E / (kdim * epsilon)
    me_n = lax.axis_index("noise")
    me_d = lax.axis_index("dp")
    me_y, me_z = me_d // zs, me_d % zs

    def peer_noise(step):
        return ((me_n + step) % n_noise, me_d)

    def peer_y(step):
        return (me_n, (me_y + step) % ys * zs + me_z)

    def peer_z(step):
        return (me_n, me_y * zs + (me_z + step) % zs)

    barrier = pltpu.get_barrier_semaphore()

    def greet_noise(k, carry):
        pl.semaphore_signal(barrier, inc=1, device_id=peer_noise(k), device_id_type=MESH)
        return carry

    def greet_y(k, carry):
        pl.semaphore_signal(barrier, inc=1, device_id=peer_y(k), device_id_type=MESH)
        return carry

    def greet_z(k, carry):
        pl.semaphore_signal(barrier, inc=1, device_id=peer_z(k), device_id_type=MESH)
        return carry

    lax.fori_loop(1, n_noise, greet_noise, 0)
    lax.fori_loop(1, ys, greet_y, 0)
    lax.fori_loop(1, zs, greet_z, 0)

    proj2_ref[0:kdim, :] = proj_ref[...]
    proj2_ref[kdim : 2 * kdim, :] = proj_ref[...]
    half = jnp.full((8, LANES), 0.5, jnp.bfloat16)
    one = jnp.ones((1, LANES), jnp.float32)
    zero = jnp.zeros((2, LANES), jnp.float32)

    def put_bias(dst_ref, c, bias, first):
        parts = list(split3(bias))
        ones = [one, one, one]
        tile = jnp.concatenate((parts + ones if first else ones + parts) + [zero], axis=0)
        dst_ref[c * LANES : (c + 1) * LANES, 128:136] = tile.T.astype(jnp.bfloat16)

    def prepare(src_ref, dst_ref, bias_ref, count, is_q):
        step = min(512, count)

        def body(b, carry):
            sl = pl.ds(pl.multiple_of(b * step, step), step)
            proj = lax.dot_general(
                src_ref[sl, :], proj2_ref[...], NT, preferred_element_type=jnp.float32
            )
            code = proj.astype(jnp.bfloat16)
            full = code.astype(jnp.float32)
            square = full * full
            sq_hi = square.astype(jnp.bfloat16)
            sq_lo = (square - sq_hi.astype(jnp.float32)).astype(jnp.bfloat16)
            norm = lax.dot_general(
                half, sq_hi, NT, preferred_element_type=jnp.float32
            ) + lax.dot_general(half, sq_lo, NT, preferred_element_type=jnp.float32)
            if is_q:
                dst_ref[sl, 0:128] = code
            else:
                scaled = full * scale
                hi = scaled.astype(jnp.bfloat16)
                lo = (scaled - hi.astype(jnp.float32)).astype(jnp.bfloat16)
                lane = lax.broadcasted_iota(jnp.int32, scaled.shape, 1)
                dst_ref[sl, 0:128] = jnp.where(
                    lane < kdim, hi.astype(jnp.float32), lo.astype(jnp.float32)
                ).astype(jnp.bfloat16)
            dst_ref[sl, 128:256] = jnp.zeros((step, 128), jnp.bfloat16)
            for c in range(step // LANES):
                bias_ref[pl.ds(b * (step // LANES) + c, 1), :] = (
                    -norm_scale * norm[0:1, c * LANES : (c + 1) * LANES]
                )
            return carry

        lax.fori_loop(0, count // step, body, 0)
        bias = bias_ref[...]
        for c in range(count // LANES):
            put_bias(dst_ref, c, bias[c : c + 1, :], is_q)

    prepare(noise_ref, q_ref, ul_ref, rows, True)
    prepare(data_ref, r_ref, vl_ref, cols, False)

    def lse_pass(lhs_ref, count, rhs_ref, width, write):
        bw = min(2048, width)
        bl = 256
        un = min(4, count // bl)

        def wide(w, carry):
            rhs = rhs_ref[pl.ds(pl.multiple_of(w * bw, bw), bw), :]

            def body(step, state):
                top, total = state
                for u in range(un):
                    sl = pl.ds(pl.multiple_of((step * un + u) * bl, bl), bl)
                    z = lax.dot_general(
                        lhs_ref[sl, :], rhs, NT, preferred_element_type=jnp.float32
                    ).reshape(bl // 8, 8, bw)
                    new = jnp.maximum(top, jnp.max(z, axis=0))
                    total = total * jnp.exp2(top - new) + jnp.sum(jnp.exp2(z - new[None]), axis=0)
                    top = new
                return top, total

            start = (jnp.full((8, bw), -1e30, jnp.float32), jnp.zeros((8, bw), jnp.float32))
            top, total = lax.fori_loop(0, count // (bl * un), body, start)
            best = jnp.max(top, axis=0, keepdims=True)
            write(w, bw, best, jnp.sum(total * jnp.exp2(top - best), axis=0, keepdims=True))
            return carry

        lax.fori_loop(0, width // bw, wide, 0)

    def gather(ref, sem, size, me, peer):
        def copy(k):
            return pltpu.make_async_remote_copy(
                src_ref=ref.at[me],
                dst_ref=ref.at[me],
                send_sem=sem.at[0, k],
                recv_sem=sem.at[1, me],
                device_id=peer(k),
                device_id_type=MESH,
            )

        def start(k, carry):
            copy(k).start()
            return carry

        def wait(k, carry):
            source = (me + size - k) % size
            pltpu.make_async_copy(ref.at[source], ref.at[source], sem.at[1, source]).wait()
            copy(k).wait_send()
            return carry

        lax.fori_loop(1, size, start, 0)
        return lambda: lax.fori_loop(1, size, wait, 0)

    def joined(ref, size):
        top = ref[0]
        for k in range(1, size):
            top = jnp.maximum(top, ref[k])
        total = jnp.exp2(ref[0] - top)
        for k in range(1, size):
            total = total + jnp.exp2(ref[k] - top)
        return top + jnp.log(total) * LOG2E

    def write1(w, bw, top, total):
        lse = top + jnp.log(total) * LOG2E
        for c in range(bw // LANES):
            put = pl.ds(w * (bw // LANES) + c, 1)
            st1_ref[me_n, put, :] = lse[:, c * LANES : (c + 1) * LANES]

    def write2(w, bw, top, total):
        lse = top + jnp.log(total) * LOG2E
        for c in range(bw // LANES):
            put = pl.ds(w * (bw // LANES) + c, 1)
            lse_ref[put, :] = lse[:, c * LANES : (c + 1) * LANES]

    lse_pass(q_ref, rows, r_ref, cols, write1)
    pl.semaphore_wait(barrier, n_noise - 1 + ys - 1 + zs - 1)

    gather(st1_ref, s1_sem, n_noise, me_n, peer_noise)()
    g1 = log_rows - joined(st1_ref, n_noise)
    vl = vl_ref[...] + g1
    for c in range(cch):
        put_bias(r_ref, c, vl[c : c + 1, :], False)

    lse_pass(r_ref, cols, q_ref, rows, write2)

    bl, bw, un = 256, cols, min(4, rows // 256)
    per = bl // LANES

    def weights(step, carry):
        for u in range(un):
            tile = step * un + u
            sl = pl.ds(pl.multiple_of(tile * bl, bl), bl)
            z = lax.dot_general(q_ref[sl, :], r_ref[...], NT, preferred_element_type=jnp.float32)
            p = jnp.exp2(z).astype(jnp.bfloat16)
            for i in range(per):
                chunk = tile * per + i
                put = pl.ds(pl.multiple_of(chunk // zs * LANES, LANES), LANES)
                p_ref[chunk % zs, put, :] = p[i * LANES : (i + 1) * LANES]
        return carry

    hch = rch // 2
    steps = rows // (bl * un)
    gy1_ref[me_y] = lse_ref[0:hch]
    gz2_ref[me_z] = lse_ref[hch:rch]
    wait_y = gather(gy1_ref, gy1_sem, ys, me_y, peer_y)
    wait_z = gather(gz2_ref, gz2_sem, zs, me_z, peer_z)
    lse = lse_ref[...]
    ul = ul_ref[...] - lse
    for c in range(rch):
        put_bias(q_ref, c, ul[c : c + 1, :], True)
    lax.fori_loop(0, steps // 2, weights, 0)
    wait_y()
    gz1_ref[me_z] = joined(gy1_ref, ys)
    wait_y = gather(gz1_ref, gz1_sem, zs, me_z, peer_z)
    wait_z()
    gy2_ref[me_y] = joined(gz2_ref, zs)
    wait_z = gather(gy2_ref, gy2_sem, ys, me_y, peer_y)
    lax.fori_loop(steps // 2, steps, weights, 0)
    wait_y()
    rho_ref[0:hch] = jnp.exp2(lse[0:hch] - joined(gz1_ref, zs) + log_cols)
    wait_z()
    rho_ref[hch:rch] = jnp.exp2(lse[hch:rch] - joined(gy2_ref, ys) + log_cols)

    rho = rho_ref[...]
    rho_hi = rho.astype(jnp.bfloat16).astype(jnp.float32)
    rho_lo = rho - rho_hi
    zero6 = jnp.zeros((6, ys * LANES), jnp.float32)
    total = jnp.zeros((8, cols), jnp.float32)
    for z in range(zs):
        lines = []
        for part in (rho_hi, rho_lo):
            lines.append(
                jnp.concatenate([part[y * zs + z : y * zs + z + 1] for y in range(ys)], axis=1)
            )
        lhs = jnp.concatenate(lines + [zero6], axis=0).astype(jnp.bfloat16)
        total = total + jnp.dot(lhs, p_ref[z], preferred_element_type=jnp.float32)
    total = total[0:1] + total[1:2]
    for c in range(cch):
        st3_ref[me_n, c : c + 1, :] = total[:, c * LANES : (c + 1) * LANES]
    gather(st3_ref, s3_sem, n_noise, me_n, peer_noise)()
    total = st3_ref[0]
    for k in range(1, n_noise):
        total = total + st3_ref[k]
    pot_ref[...] = (epsilon * LN2) * (g1 + log_rows - jnp.log(total) * LOG2E)

    factor = float(rows * n_noise) / total
    f_hi = factor.astype(jnp.bfloat16).astype(jnp.float32)
    f_lo = factor - f_hi
    zero5 = jnp.zeros((5, LANES), jnp.float32)
    for c in range(cch):
        sl = slice(c * LANES, (c + 1) * LANES)
        tile = jnp.concatenate(
            [f_hi[c : c + 1], f_lo[c : c + 1], factor[c : c + 1], zero5], axis=0
        ).T
        d_ref[sl, 0:128] = (data_ref[sl, :].astype(jnp.float32) * tile[:, 2:3]).astype(
            jnp.bfloat16
        )
        d_ref[sl, 128:256] = jnp.zeros((LANES, 128), jnp.bfloat16)
        d_ref[sl, 128:136] = tile.astype(jnp.bfloat16)

    h = zs // 2
    offsets = [h]
    for k in range(h - 1, 0, -1):
        offsets += [k, zs - k]
    offsets.append(0)
    pending = []
    cuts = (pl.ds(0, 72), pl.ds(72, 64))

    def send(src, dst, sem, device):
        copy = pltpu.make_async_remote_copy(
            src_ref=src,
            dst_ref=dst,
            send_sem=sem.at[0],
            recv_sem=sem.at[1],
            device_id=device,
            device_id_type=MESH,
        )
        copy.start()
        pending.append(copy)

    def arrived(ref, sem):
        pltpu.make_async_copy(ref, ref, sem.at[1]).wait()

    def weigh(off):
        zt = (me_z + off) % zs
        both = jnp.dot(p_ref[zt], d_ref[...], preferred_element_type=jnp.float32)
        for y in range(ys):
            line = rho_ref[pl.ds(y * zs + zt, 1), :]
            column = jnp.broadcast_to(line, (8, LANES)).T[:, 0:1]
            part = both[y * LANES : (y + 1) * LANES] * column
            num_ref[zt, y, 0:64, :] = part[0:64, 0:128]
            num_ref[zt, y, 64:72, :] = part[:, 128:136].T
            num_ref[zt, y, 72:136, :] = part[64:128, 0:128]

    def along(way, step):
        return (me_y + (step if way == 0 else ys - step)) % ys

    def y_send(i):
        zt = (me_z + offsets[i]) % zs
        if ys == 4:
            for way in range(2):
                send(
                    num_ref.at[zt, along(way, 2), cuts[way]],
                    far_ref.at[i, cuts[way]],
                    far_sem.at[i, way],
                    peer_y(1 if way == 0 else ys - 1),
                )
        for way in range(2):
            send(
                num_ref.at[zt, along(way, 1), cuts[1 - way]],
                near_ref.at[way, i, cuts[1 - way]],
                near_sem.at[way, i, 0],
                peer_y(1 if way == 0 else ys - 1),
            )

    def y_forward(i):
        if ys != 4:
            return
        zt = (me_z + offsets[i]) % zs
        for way in range(2):
            arrived(far_ref.at[i, cuts[way]], far_sem.at[i, way])
            to = along(way, 1)
            num_ref[zt, to, cuts[way]] = num_ref[zt, to, cuts[way]] + far_ref[i, cuts[way]]
            send(
                num_ref.at[zt, to, cuts[way]],
                near_ref.at[way, i, cuts[way]],
                near_sem.at[way, i, 1],
                peer_y(1 if way == 0 else ys - 1),
            )

    def y_merge(i):
        zt = (me_z + offsets[i]) % zs
        for way in range(2):
            arrived(near_ref.at[way, i, cuts[1 - way]], near_sem.at[way, i, 0])
            if ys == 4:
                arrived(near_ref.at[way, i, cuts[way]], near_sem.at[way, i, 1])
        if ys == 4:
            num_ref[zt, me_y] = num_ref[zt, me_y] + near_ref[0, i] + near_ref[1, i]
        else:
            for way in range(2):
                part = cuts[1 - way]
                num_ref[zt, me_y, part] = num_ref[zt, me_y, part] + near_ref[way, i, part]
        if offsets[i]:
            send(num_ref.at[zt, me_y], rz_ref.at[i], rz_sem.at[i], peer_z(offsets[i]))

    lag = zs // 2
    for i in range(zs):
        weigh(offsets[i])
        y_send(i)
        if i >= lag:
            y_forward(i - lag)
    for i in range(lag):
        y_forward(zs - lag + i)
        y_merge(i)
    for i in range(lag, zs):
        y_merge(i)
    mine = num_ref[me_z, me_y]
    for i in range(zs - 1):
        arrived(rz_ref.at[i], rz_sem.at[i])
        mine = mine + rz_ref[i]
    den = (mine[64:72]).T
    den = den[:, 0:1] + den[:, 1:2]
    targets_ref[0:64, :] = mine[0:64] / den[0:64]
    targets_ref[64:128, :] = mine[72:136] / den[64:128]
    for copy in pending:
        copy.wait_send()


def shards(noise_latents, data_latents, projection):
    rows, width = noise_latents.shape
    cols = data_latents.shape[0]
    kdim = projection.shape[1]
    n_noise, n_dp = lax.axis_size("noise"), lax.axis_size("dp")
    ys, zs = ring_sizes(n_dp)
    rch, cch = rows // LANES, cols // LANES
    f32, bf16 = jnp.float32, jnp.bfloat16
    cfg = (rows, cols, n_noise, n_dp, kdim)
    dma = pltpu.SemaphoreType.DMA
    vmem = pl.BlockSpec(memory_space=pltpu.VMEM)
    targets, pot = pl.pallas_call(
        functools.partial(kernel, cfg),
        out_shape=(
            jax.ShapeDtypeStruct((LANES, width), f32),
            jax.ShapeDtypeStruct((cch, LANES), f32),
        ),
        in_specs=[vmem] * 3,
        out_specs=(vmem, vmem),
        scratch_shapes=[
            pltpu.VMEM((rows, 256), bf16),
            pltpu.VMEM((cols, 256), bf16),
            pltpu.VMEM((zs, ys * LANES, cols), bf16),
            pltpu.VMEM((cols, 256), bf16),
            pltpu.VMEM((2 * kdim, width), bf16),
            pltpu.VMEM((rch, LANES), f32),
            pltpu.VMEM((cch, LANES), f32),
            pltpu.VMEM((n_noise, cch, LANES), f32),
            pltpu.VMEM((rch, LANES), f32),
            pltpu.VMEM((rch, LANES), f32),
            pltpu.VMEM((ys, rch // 2, LANES), f32),
            pltpu.VMEM((zs, rch // 2, LANES), f32),
            pltpu.VMEM((zs, rch // 2, LANES), f32),
            pltpu.VMEM((ys, rch // 2, LANES), f32),
            pltpu.VMEM((n_noise, cch, LANES), f32),
            pltpu.VMEM((zs, ys, 136, LANES), f32),
            pltpu.VMEM((zs, 136, LANES), f32),
            pltpu.VMEM((2, zs, 136, LANES), f32),
            pltpu.VMEM((zs - 1, 136, LANES), f32),
            dma((2, n_noise)),
            dma((2, n_noise)),
            dma((2, ys)),
            dma((2, zs)),
            dma((2, zs)),
            dma((2, ys)),
            dma((zs, 2, 2)),
            dma((2, zs, 2, 2)),
            dma((zs - 1, 2)),
        ],
        compiler_params=pltpu.CompilerParams(
            collective_id=0, has_side_effects=True, vmem_limit_bytes=56 * 2**20
        ),
        cost_estimate=pl.CostEstimate(
            flops=8 * rows * cols * 256, bytes_accessed=2**21, transcendentals=3 * rows * cols
        ),
    )(noise_latents, data_latents, projection.T)
    return (targets, pot.reshape(cols))


def solution(mesh):
    in_specs = (P("noise", None), P("dp", None), P())
    out_specs = (P(("noise", "dp"), None), P("dp"))
    return jax.shard_map(shards, mesh=mesh, in_specs=in_specs, out_specs=out_specs, check_vma=False)
```

```python
import functools
import math

import jax
import jax.numpy as jnp
from jax import lax
from jax.experimental import pallas as pl
from jax.experimental.pallas import tpu as pltpu
from jax.sharding import PartitionSpec as P

epsilon = 0.02
LOG2E = 1.0 / math.log(2.0)
LN2 = math.log(2.0)
NT = (((1,), (1,)), ((), ()))
MESH = pl.DeviceIdType.MESH
LANES = 128


def ring_sizes(dp):
    return {32: (4, 8), 8: (2, 4), 16: (4, 4)}[dp]


def split3(x):
    hi = x.astype(jnp.bfloat16).astype(jnp.float32)
    rest = x - hi
    mid = rest.astype(jnp.bfloat16).astype(jnp.float32)
    return hi, mid, rest - mid


def kernel(
    cfg,
    noise_ref,
    data_ref,
    proj_ref,
    targets_ref,
    pot_ref,
    q_ref,
    r_ref,
    p_ref,
    d_ref,
    proj2_ref,
    ul_ref,
    vl_ref,
    st1a_ref,
    st1b_ref,
    lsea_ref,
    lseb_ref,
    rho_ref,
    gy_ref,
    gz_ref,
    st3_ref,
    num_ref,
    far_ref,
    near_ref,
    rz_ref,
    s1_sem,
    s3_sem,
    gy_sem,
    gz_sem,
    far_sem,
    near_sem,
    rz_sem,
):
    rows, cols, n_noise, n_dp, kdim = cfg
    ys, zs = ring_sizes(n_dp)
    rch, cch = rows // LANES, cols // LANES
    log_rows = math.log2(rows * n_noise)
    log_cols = math.log2(cols * n_dp)
    scale = 2.0 * LOG2E / (kdim * epsilon)
    norm_scale = LOG2E / (kdim * epsilon)
    me_n = lax.axis_index("noise")
    me_d = lax.axis_index("dp")
    me_y, me_z = me_d // zs, me_d % zs

    def peer_noise(step):
        return ((me_n + step) % n_noise, me_d)

    def peer_y(step):
        return (me_n, (me_y + step) % ys * zs + me_z)

    def peer_z(step):
        return (me_n, me_y * zs + (me_z + step) % zs)

    barrier = pltpu.get_barrier_semaphore()

    def greet_noise(k, carry):
        pl.semaphore_signal(barrier, inc=1, device_id=peer_noise(k), device_id_type=MESH)
        return carry

    def greet_y(k, carry):
        pl.semaphore_signal(barrier, inc=1, device_id=peer_y(k), device_id_type=MESH)
        return carry

    def greet_z(k, carry):
        pl.semaphore_signal(barrier, inc=1, device_id=peer_z(k), device_id_type=MESH)
        return carry

    lax.fori_loop(1, n_noise, greet_noise, 0)
    lax.fori_loop(1, ys, greet_y, 0)
    lax.fori_loop(1, zs, greet_z, 0)

    proj2_ref[0:kdim, :] = proj_ref[...]
    proj2_ref[kdim : 2 * kdim, :] = proj_ref[...]
    half = jnp.full((8, LANES), 0.5, jnp.bfloat16)
    one = jnp.ones((1, LANES), jnp.float32)
    zero = jnp.zeros((2, LANES), jnp.float32)

    def put_bias(dst_ref, c, bias, first):
        parts = list(split3(bias))
        ones = [one, one, one]
        tile = jnp.concatenate((parts + ones if first else ones + parts) + [zero], axis=0)
        dst_ref[c * LANES : (c + 1) * LANES, 128:136] = tile.T.astype(jnp.bfloat16)

    def prepare(src_ref, dst_ref, bias_ref, count, is_q):
        step = min(2048, count)

        def body(b, carry):
            sl = pl.ds(pl.multiple_of(b * step, step), step)
            proj = lax.dot_general(
                src_ref[sl, :], proj2_ref[...], NT, preferred_element_type=jnp.float32
            )
            code = proj.astype(jnp.bfloat16)
            full = code.astype(jnp.float32)
            square = full * full
            sq_hi = square.astype(jnp.bfloat16)
            sq_lo = (square - sq_hi.astype(jnp.float32)).astype(jnp.bfloat16)
            norm = lax.dot_general(
                half, sq_hi, NT, preferred_element_type=jnp.float32
            ) + lax.dot_general(half, sq_lo, NT, preferred_element_type=jnp.float32)
            if is_q:
                dst_ref[sl, 0:128] = code
            else:
                scaled = full * scale
                hi = scaled.astype(jnp.bfloat16)
                lo = (scaled - hi.astype(jnp.float32)).astype(jnp.bfloat16)
                lane = lax.broadcasted_iota(jnp.int32, scaled.shape, 1)
                dst_ref[sl, 0:128] = jnp.where(
                    lane < kdim, hi.astype(jnp.float32), lo.astype(jnp.float32)
                ).astype(jnp.bfloat16)
            dst_ref[sl, 128:256] = jnp.zeros((step, 128), jnp.bfloat16)
            for c in range(step // LANES):
                bias_ref[pl.ds(b * (step // LANES) + c, 1), :] = (
                    -norm_scale * norm[0:1, c * LANES : (c + 1) * LANES]
                )
            return carry

        lax.fori_loop(0, count // step, body, 0)
        bias = bias_ref[...]
        for c in range(count // LANES):
            put_bias(dst_ref, c, bias[c : c + 1, :], is_q)

    prepare(noise_ref, q_ref, ul_ref, rows, True)
    prepare(data_ref, r_ref, vl_ref, cols, False)

    def lse_pass(lhs_ref, first, count, rhs_ref, start, width, write):
        bw = min(2048, width)
        bl = 256
        un = max(1, min(2**21 // (bl * bw), count // bl))

        def wide(w, carry):
            rhs = rhs_ref[pl.ds(pl.multiple_of(start + w * bw, bw), bw), :]

            def body(step, state):
                top, total = state
                for u in range(un):
                    sl = pl.ds(pl.multiple_of(first + (step * un + u) * bl, bl), bl)
                    z = lax.dot_general(
                        lhs_ref[sl, :], rhs, NT, preferred_element_type=jnp.float32
                    ).reshape(bl // 8, 8, bw)
                    new = jnp.maximum(top, jnp.max(z, axis=0))
                    total = total * jnp.exp2(top - new) + jnp.sum(jnp.exp2(z - new[None]), axis=0)
                    top = new
                return top, total

            state = (jnp.full((8, bw), -1e30, jnp.float32), jnp.zeros((8, bw), jnp.float32))
            top, total = lax.fori_loop(0, count // (bl * un), body, state)
            best = jnp.max(top, axis=0, keepdims=True)
            total = jnp.sum(total * jnp.exp2(top - best), axis=0, keepdims=True)
            lse = best + jnp.log(total) * LOG2E
            for c in range(bw // LANES):
                write(w * (bw // LANES) + c, lse[:, c * LANES : (c + 1) * LANES])
            return carry

        lax.fori_loop(0, width // bw, wide, 0)

    def gather(ref, sem, size, me, peer):
        def copy(k):
            return pltpu.make_async_remote_copy(
                src_ref=ref.at[me],
                dst_ref=ref.at[me],
                send_sem=sem.at[0, k],
                recv_sem=sem.at[1, me],
                device_id=peer(k),
                device_id_type=MESH,
            )

        def start(k, carry):
            copy(k).start()
            return carry

        def wait(k, carry):
            source = (me + size - k) % size
            pltpu.make_async_copy(ref.at[source], ref.at[source], sem.at[1, source]).wait()
            copy(k).wait_send()
            return carry

        lax.fori_loop(1, size, start, 0)
        return lambda: lax.fori_loop(1, size, wait, 0)

    def joined(ref, size):
        top = ref[0]
        for k in range(1, size):
            top = jnp.maximum(top, ref[k])
        total = jnp.exp2(ref[0] - top)
        for k in range(1, size):
            total = total + jnp.exp2(ref[k] - top)
        return top + jnp.log(total) * LOG2E

    hcol, hch = cols // 2, cch // 2
    waits, g1 = [], []
    for i, ref in enumerate((st1a_ref, st1b_ref)):

        def write(chunk, line):
            ref[me_n, pl.ds(chunk, 1), :] = line

        lse_pass(q_ref, 0, rows, r_ref, i * hcol, hcol, write)
        if i == 0:
            pl.semaphore_wait(barrier, n_noise - 1 + ys - 1 + zs - 1)
        waits.append(gather(ref, s1_sem.at[i], n_noise, me_n, peer_noise))
    for i, (ref, out_ref) in enumerate(((st1a_ref, lsea_ref), (st1b_ref, lseb_ref))):
        waits[i]()
        g1.append(log_rows - joined(ref, n_noise))
        vl = vl_ref[i * hch : (i + 1) * hch] + g1[i]
        for c in range(hch):
            put_bias(r_ref, i * hch + c, vl[c : c + 1, :], False)

        def write(chunk, line):
            out_ref[pl.ds(chunk, 1), :] = line

        lse_pass(r_ref, i * hcol, hcol, q_ref, 0, rows, write)
    g1 = jnp.concatenate(g1, axis=0)

    bl, bw, un = 256, cols, min(4, rows // 256)
    per = bl // LANES

    def weights(step, carry):
        for u in range(un):
            tile = step * un + u
            sl = pl.ds(pl.multiple_of(tile * bl, bl), bl)
            z = lax.dot_general(q_ref[sl, :], r_ref[...], NT, preferred_element_type=jnp.float32)
            p = jnp.exp2(z).astype(jnp.bfloat16)
            for i in range(per):
                chunk = tile * per + i
                put = pl.ds(pl.multiple_of(chunk // zs * LANES, LANES), LANES)
                p_ref[chunk % zs, put, :] = p[i * LANES : (i + 1) * LANES]
        return carry

    steps = rows // (bl * un)
    top = jnp.maximum(lsea_ref[...], lseb_ref[...])
    lse = top + LOG2E * jnp.log(jnp.exp2(lsea_ref[...] - top) + jnp.exp2(lseb_ref[...] - top))
    gy_ref[me_y] = lse
    wait = gather(gy_ref, gy_sem, ys, me_y, peer_y)
    ul = ul_ref[...] - lse
    for c in range(rch):
        put_bias(q_ref, c, ul[c : c + 1, :], True)
    lax.fori_loop(0, steps // 2, weights, 0)
    wait()
    gz_ref[me_z] = joined(gy_ref, ys)
    wait = gather(gz_ref, gz_sem, zs, me_z, peer_z)
    lax.fori_loop(steps // 2, steps, weights, 0)
    wait()
    rho_ref[...] = jnp.exp2(lse - joined(gz_ref, zs) + log_cols)

    rho = rho_ref[...]
    rho_hi = rho.astype(jnp.bfloat16).astype(jnp.float32)
    rho_lo = rho - rho_hi
    zero6 = jnp.zeros((6, ys * LANES), jnp.float32)
    total = jnp.zeros((8, cols), jnp.float32)
    for z in range(zs):
        lines = []
        for part in (rho_hi, rho_lo):
            lines.append(
                jnp.concatenate([part[y * zs + z : y * zs + z + 1] for y in range(ys)], axis=1)
            )
        lhs = jnp.concatenate(lines + [zero6], axis=0).astype(jnp.bfloat16)
        total = total + jnp.dot(lhs, p_ref[z], preferred_element_type=jnp.float32)
    total = total[0:1] + total[1:2]
    for c in range(cch):
        st3_ref[me_n, c : c + 1, :] = total[:, c * LANES : (c + 1) * LANES]
    gather(st3_ref, s3_sem, n_noise, me_n, peer_noise)()
    total = st3_ref[0]
    for k in range(1, n_noise):
        total = total + st3_ref[k]
    pot_ref[...] = (epsilon * LN2) * (g1 + log_rows - jnp.log(total) * LOG2E)

    factor = float(rows * n_noise) / total
    f_hi = factor.astype(jnp.bfloat16).astype(jnp.float32)
    f_lo = factor - f_hi
    zero5 = jnp.zeros((5, LANES), jnp.float32)
    for c in range(cch):
        sl = slice(c * LANES, (c + 1) * LANES)
        tile = jnp.concatenate(
            [f_hi[c : c + 1], f_lo[c : c + 1], factor[c : c + 1], zero5], axis=0
        ).T
        d_ref[sl, 0:128] = (data_ref[sl, :].astype(jnp.float32) * tile[:, 2:3]).astype(
            jnp.bfloat16
        )
        d_ref[sl, 128:256] = jnp.zeros((LANES, 128), jnp.bfloat16)
        d_ref[sl, 128:136] = tile.astype(jnp.bfloat16)

    h = zs // 2
    offsets = [h]
    for k in range(h - 1, 0, -1):
        offsets += [k, zs - k]
    offsets.append(0)
    pending = []
    cuts = (pl.ds(0, 72), pl.ds(72, 64))

    def send(src, dst, sem, device):
        copy = pltpu.make_async_remote_copy(
            src_ref=src,
            dst_ref=dst,
            send_sem=sem.at[0],
            recv_sem=sem.at[1],
            device_id=device,
            device_id_type=MESH,
        )
        copy.start()
        pending.append(copy)

    def arrived(ref, sem):
        pltpu.make_async_copy(ref, ref, sem.at[1]).wait()

    def weigh(off):
        zt = (me_z + off) % zs
        both = jnp.dot(p_ref[zt], d_ref[...], preferred_element_type=jnp.float32)
        for y in range(ys):
            line = rho_ref[pl.ds(y * zs + zt, 1), :]
            column = jnp.broadcast_to(line, (8, LANES)).T[:, 0:1]
            part = both[y * LANES : (y + 1) * LANES] * column
            num_ref[zt, y, 0:64, :] = part[0:64, 0:128]
            num_ref[zt, y, 64:72, :] = part[:, 128:136].T
            num_ref[zt, y, 72:136, :] = part[64:128, 0:128]

    def along(way, step):
        return (me_y + (step if way == 0 else ys - step)) % ys

    def y_far(i):
        zt = (me_z + offsets[i]) % zs
        if ys == 4:
            for way in range(2):
                send(
                    num_ref.at[zt, along(way, 2), cuts[way]],
                    far_ref.at[i, cuts[way]],
                    far_sem.at[i, way],
                    peer_y(1 if way == 0 else ys - 1),
                )

    def y_near(i):
        zt = (me_z + offsets[i]) % zs
        for way in range(2):
            send(
                num_ref.at[zt, along(way, 1), cuts[1 - way]],
                near_ref.at[way, i, cuts[1 - way]],
                near_sem.at[way, i, 0],
                peer_y(1 if way == 0 else ys - 1),
            )

    def y_forward(i):
        if ys != 4:
            return
        zt = (me_z + offsets[i]) % zs
        for way in range(2):
            arrived(far_ref.at[i, cuts[way]], far_sem.at[i, way])
            to = along(way, 1)
            num_ref[zt, to, cuts[way]] = num_ref[zt, to, cuts[way]] + far_ref[i, cuts[way]]
            send(
                num_ref.at[zt, to, cuts[way]],
                near_ref.at[way, i, cuts[way]],
                near_sem.at[way, i, 1],
                peer_y(1 if way == 0 else ys - 1),
            )

    def y_merge(i):
        zt = (me_z + offsets[i]) % zs
        for way in range(2):
            arrived(near_ref.at[way, i, cuts[1 - way]], near_sem.at[way, i, 0])
            if ys == 4:
                arrived(near_ref.at[way, i, cuts[way]], near_sem.at[way, i, 1])
        if ys == 4:
            num_ref[zt, me_y] = num_ref[zt, me_y] + near_ref[0, i] + near_ref[1, i]
        else:
            for way in range(2):
                part = cuts[1 - way]
                num_ref[zt, me_y, part] = num_ref[zt, me_y, part] + near_ref[way, i, part]
        if offsets[i]:
            send(num_ref.at[zt, me_y], rz_ref.at[i], rz_sem.at[i], peer_z(offsets[i]))

    for i in range(zs):
        weigh(offsets[i])
        y_far(i)
    for i in range(zs):
        y_near(i)
        y_forward(i)
    for i in range(zs):
        y_merge(i)
    mine = num_ref[me_z, me_y]
    for i in range(zs - 1):
        arrived(rz_ref.at[i], rz_sem.at[i])
        mine = mine + rz_ref[i]
    den = (mine[64:72]).T
    den = den[:, 0:1] + den[:, 1:2]
    targets_ref[0:64, :] = mine[0:64] / den[0:64]
    targets_ref[64:128, :] = mine[72:136] / den[64:128]
    for copy in pending:
        copy.wait_send()


def shards(noise_latents, data_latents, projection):
    rows, width = noise_latents.shape
    cols = data_latents.shape[0]
    kdim = projection.shape[1]
    n_noise, n_dp = lax.axis_size("noise"), lax.axis_size("dp")
    ys, zs = ring_sizes(n_dp)
    rch, cch = rows // LANES, cols // LANES
    f32, bf16 = jnp.float32, jnp.bfloat16
    cfg = (rows, cols, n_noise, n_dp, kdim)
    dma = pltpu.SemaphoreType.DMA
    vmem = pl.BlockSpec(memory_space=pltpu.VMEM)
    targets, pot = pl.pallas_call(
        functools.partial(kernel, cfg),
        out_shape=(
            jax.ShapeDtypeStruct((LANES, width), f32),
            jax.ShapeDtypeStruct((cch, LANES), f32),
        ),
        in_specs=[vmem] * 3,
        out_specs=(vmem, vmem),
        scratch_shapes=[
            pltpu.VMEM((rows, 256), bf16),
            pltpu.VMEM((cols, 256), bf16),
            pltpu.VMEM((zs, ys * LANES, cols), bf16),
            pltpu.VMEM((cols, 256), bf16),
            pltpu.VMEM((2 * kdim, width), bf16),
            pltpu.VMEM((rch, LANES), f32),
            pltpu.VMEM((cch, LANES), f32),
            pltpu.VMEM((n_noise, cch // 2, LANES), f32),
            pltpu.VMEM((n_noise, cch // 2, LANES), f32),
            pltpu.VMEM((rch, LANES), f32),
            pltpu.VMEM((rch, LANES), f32),
            pltpu.VMEM((rch, LANES), f32),
            pltpu.VMEM((ys, rch, LANES), f32),
            pltpu.VMEM((zs, rch, LANES), f32),
            pltpu.VMEM((n_noise, cch, LANES), f32),
            pltpu.VMEM((zs, ys, 136, LANES), f32),
            pltpu.VMEM((zs, 136, LANES), f32),
            pltpu.VMEM((2, zs, 136, LANES), f32),
            pltpu.VMEM((zs - 1, 136, LANES), f32),
            dma((2, 2, n_noise)),
            dma((2, n_noise)),
            dma((2, ys)),
            dma((2, zs)),
            dma((zs, 2, 2)),
            dma((2, zs, 2, 2)),
            dma((zs - 1, 2)),
        ],
        compiler_params=pltpu.CompilerParams(
            collective_id=0, has_side_effects=True, vmem_limit_bytes=56 * 2**20
        ),
        cost_estimate=pl.CostEstimate(
            flops=8 * rows * cols * 256, bytes_accessed=2**21, transcendentals=3 * rows * cols
        ),
    )(noise_latents, data_latents, projection.T)
    return (targets, pot.reshape(cols))


def solution(mesh):
    in_specs = (P("noise", None), P("dp", None), P())
    out_specs = (P(("noise", "dp"), None), P("dp"))
    return jax.shard_map(shards, mesh=mesh, in_specs=in_specs, out_specs=out_specs, check_vma=False)
```

```python
import functools
import math

import jax
import jax.numpy as jnp
from jax import lax
from jax.experimental import pallas as pl
from jax.experimental.pallas import tpu as pltpu
from jax.sharding import PartitionSpec as P

epsilon = 0.02
LOG2E = 1.0 / math.log(2.0)
LN2 = math.log(2.0)
NT = (((1,), (1,)), ((), ()))
MESH = pl.DeviceIdType.MESH
LANES = 128


def ring_sizes(dp):
    return {32: (4, 8), 8: (2, 4), 16: (4, 4)}[dp]


def split3(x):
    hi = x.astype(jnp.bfloat16).astype(jnp.float32)
    rest = x - hi
    mid = rest.astype(jnp.bfloat16).astype(jnp.float32)
    return hi, mid, rest - mid


def kernel(
    cfg,
    noise_ref,
    data_ref,
    proj_ref,
    targets_ref,
    pot_ref,
    q_ref,
    r_ref,
    p_ref,
    d_ref,
    proj2_ref,
    ul_ref,
    vl_ref,
    st1a_ref,
    st1b_ref,
    lsea_ref,
    lseb_ref,
    lse_ref,
    rho_ref,
    gya_ref,
    gyb_ref,
    gza_ref,
    gzb_ref,
    st3_ref,
    num_ref,
    far_ref,
    near_ref,
    rz_ref,
    zf_ref,
    yf_ref,
    s1_sem,
    s3_sem,
    gy_sem,
    gz_sem,
    far_sem,
    near_sem,
    rz_sem,
    zf_sem,
    yf_sem,
):
    rows, cols, n_noise, n_dp, kdim = cfg
    ys, zs = ring_sizes(n_dp)
    rch, cch = rows // LANES, cols // LANES
    log_rows = math.log2(rows * n_noise)
    log_cols = math.log2(cols * n_dp)
    scale = 2.0 * LOG2E / (kdim * epsilon)
    norm_scale = LOG2E / (kdim * epsilon)
    me_n = lax.axis_index("noise")
    me_d = lax.axis_index("dp")
    me_y, me_z = me_d // zs, me_d % zs

    def peer_noise(step):
        return ((me_n + step) % n_noise, me_d)

    def peer_y(step):
        return (me_n, (me_y + step) % ys * zs + me_z)

    def peer_z(step):
        return (me_n, me_y * zs + (me_z + step) % zs)

    barrier = pltpu.get_barrier_semaphore()

    def greet_noise(k, carry):
        pl.semaphore_signal(barrier, inc=1, device_id=peer_noise(k), device_id_type=MESH)
        return carry

    def greet_y(k, carry):
        pl.semaphore_signal(barrier, inc=1, device_id=peer_y(k), device_id_type=MESH)
        return carry

    def greet_z(k, carry):
        pl.semaphore_signal(barrier, inc=1, device_id=peer_z(k), device_id_type=MESH)
        return carry

    lax.fori_loop(1, n_noise, greet_noise, 0)
    lax.fori_loop(1, ys, greet_y, 0)
    lax.fori_loop(1, zs, greet_z, 0)

    proj2_ref[0:kdim, :] = proj_ref[...]
    proj2_ref[kdim : 2 * kdim, :] = proj_ref[...]
    half = jnp.full((8, LANES), 0.5, jnp.bfloat16)
    one = jnp.ones((1, LANES), jnp.float32)
    zero = jnp.zeros((2, LANES), jnp.float32)

    def put_bias(dst_ref, c, bias, first):
        parts = list(split3(bias))
        ones = [one, one, one]
        tile = jnp.concatenate((parts + ones if first else ones + parts) + [zero], axis=0)
        dst_ref[c * LANES : (c + 1) * LANES, 128:136] = tile.T.astype(jnp.bfloat16)

    def prepare(src_ref, dst_ref, bias_ref, count, is_q):
        step = min(2048, count)

        def body(b, carry):
            sl = pl.ds(pl.multiple_of(b * step, step), step)
            proj = lax.dot_general(
                src_ref[sl, :], proj2_ref[...], NT, preferred_element_type=jnp.float32
            )
            code = proj.astype(jnp.bfloat16)
            full = code.astype(jnp.float32)
            square = full * full
            sq_hi = square.astype(jnp.bfloat16)
            sq_lo = (square - sq_hi.astype(jnp.float32)).astype(jnp.bfloat16)
            norm = lax.dot_general(
                half, sq_hi, NT, preferred_element_type=jnp.float32
            ) + lax.dot_general(half, sq_lo, NT, preferred_element_type=jnp.float32)
            if is_q:
                dst_ref[sl, 0:128] = code
            else:
                scaled = full * scale
                hi = scaled.astype(jnp.bfloat16)
                lo = (scaled - hi.astype(jnp.float32)).astype(jnp.bfloat16)
                lane = lax.broadcasted_iota(jnp.int32, scaled.shape, 1)
                dst_ref[sl, 0:128] = jnp.where(
                    lane < kdim, hi.astype(jnp.float32), lo.astype(jnp.float32)
                ).astype(jnp.bfloat16)
            dst_ref[sl, 128:256] = jnp.zeros((step, 128), jnp.bfloat16)
            for c in range(step // LANES):
                bias_ref[pl.ds(b * (step // LANES) + c, 1), :] = (
                    -norm_scale * norm[0:1, c * LANES : (c + 1) * LANES]
                )
            return carry

        lax.fori_loop(0, count // step, body, 0)
        bias = bias_ref[...]
        for c in range(count // LANES):
            put_bias(dst_ref, c, bias[c : c + 1, :], is_q)

    prepare(noise_ref, q_ref, ul_ref, rows, True)
    prepare(data_ref, r_ref, vl_ref, cols, False)

    def lse_pass(lhs_ref, first, count, rhs_ref, start, width, write):
        bw = min(2048, width)
        bl = 256
        un = max(1, min(2**21 // (bl * bw), count // bl))

        def wide(w, carry):
            rhs = rhs_ref[pl.ds(pl.multiple_of(start + w * bw, bw), bw), :]

            def body(step, state):
                top, total = state
                for u in range(un):
                    sl = pl.ds(pl.multiple_of(first + (step * un + u) * bl, bl), bl)
                    z = lax.dot_general(
                        lhs_ref[sl, :], rhs, NT, preferred_element_type=jnp.float32
                    ).reshape(bl // 8, 8, bw)
                    new = jnp.maximum(top, jnp.max(z, axis=0))
                    total = total * jnp.exp2(top - new) + jnp.sum(jnp.exp2(z - new[None]), axis=0)
                    top = new
                return top, total

            state = (jnp.full((8, bw), -1e30, jnp.float32), jnp.zeros((8, bw), jnp.float32))
            top, total = lax.fori_loop(0, count // (bl * un), body, state)
            best = jnp.max(top, axis=0, keepdims=True)
            total = jnp.sum(total * jnp.exp2(top - best), axis=0, keepdims=True)
            lse = best + jnp.log(total) * LOG2E
            for c in range(bw // LANES):
                write(w * (bw // LANES) + c, lse[:, c * LANES : (c + 1) * LANES])
            return carry

        lax.fori_loop(0, width // bw, wide, 0)

    def gather(ref, sem, size, me, peer):
        def copy(k):
            return pltpu.make_async_remote_copy(
                src_ref=ref.at[me],
                dst_ref=ref.at[me],
                send_sem=sem.at[0, k],
                recv_sem=sem.at[1, me],
                device_id=peer(k),
                device_id_type=MESH,
            )

        def start(k, carry):
            copy(k).start()
            return carry

        def wait(k, carry):
            source = (me + size - k) % size
            pltpu.make_async_copy(ref.at[source], ref.at[source], sem.at[1, source]).wait()
            copy(k).wait_send()
            return carry

        lax.fori_loop(1, size, start, 0)
        return lambda: lax.fori_loop(1, size, wait, 0)

    def joined(ref, size):
        top = ref[0]
        for k in range(1, size):
            top = jnp.maximum(top, ref[k])
        total = jnp.exp2(ref[0] - top)
        for k in range(1, size):
            total = total + jnp.exp2(ref[k] - top)
        return top + jnp.log(total) * LOG2E

    hcol, hch = cols // 2, cch // 2
    waits, g1 = [], []
    for i, ref in enumerate((st1a_ref, st1b_ref)):

        def write(chunk, line):
            ref[me_n, pl.ds(chunk, 1), :] = line

        lse_pass(q_ref, 0, rows, r_ref, i * hcol, hcol, write)
        if i == 0:
            pl.semaphore_wait(barrier, n_noise - 1 + ys - 1 + zs - 1)
        waits.append(gather(ref, s1_sem.at[i], n_noise, me_n, peer_noise))
    hrow, rhh = rows // 2, rch // 2
    wait_y, gathered = [], ((gya_ref, gza_ref), (gyb_ref, gzb_ref))
    for i, (ref, out_ref) in enumerate(((st1a_ref, lsea_ref), (st1b_ref, lseb_ref))):
        waits[i]()
        g1.append(log_rows - joined(ref, n_noise))
        vl = vl_ref[i * hch : (i + 1) * hch] + g1[i]
        for c in range(hch):
            put_bias(r_ref, i * hch + c, vl[c : c + 1, :], False)

        def write(chunk, line):
            out_ref[pl.ds(chunk, 1), :] = line

        if i == 0:
            lse_pass(r_ref, 0, hcol, q_ref, 0, rows, write)
            continue
        for j in range(2):
            lse_pass(
                r_ref, hcol, hcol, q_ref, j * hrow, hrow, lambda c, x: write(j * rhh + c, x)
            )
            part = slice(j * rhh, (j + 1) * rhh)
            one_half, other = lsea_ref[part], lseb_ref[part]
            top = jnp.maximum(one_half, other)
            total = jnp.exp2(one_half - top) + jnp.exp2(other - top)
            lse_ref[part] = top + LOG2E * jnp.log(total)
            gathered[j][0][me_y] = lse_ref[part]
            wait_y.append(gather(gathered[j][0], gy_sem.at[j], ys, me_y, peer_y))
    g1 = jnp.concatenate(g1, axis=0)

    bl, bw, un = 256, cols, min(4, rows // 256)
    per = bl // LANES

    def weights(step, carry):
        for u in range(un):
            tile = step * un + u
            sl = pl.ds(pl.multiple_of(tile * bl, bl), bl)
            z = lax.dot_general(q_ref[sl, :], r_ref[...], NT, preferred_element_type=jnp.float32)
            p = jnp.exp2(z).astype(jnp.bfloat16)
            for i in range(per):
                chunk = tile * per + i
                put = pl.ds(pl.multiple_of(chunk // zs * LANES, LANES), LANES)
                p_ref[chunk % zs, put, :] = p[i * LANES : (i + 1) * LANES]
        return carry

    steps = rows // (bl * un)
    lse = lse_ref[...]
    ul = ul_ref[...] - lse
    for c in range(rch):
        put_bias(q_ref, c, ul[c : c + 1, :], True)
    wait_z = []
    done = 0
    for j, (y_ref, z_ref) in enumerate(gathered):
        upto = steps * (j + 1) // 4
        lax.fori_loop(done, upto, weights, 0)
        done = upto
        wait_y[j]()
        z_ref[me_z] = joined(y_ref, ys)
        wait_z.append(gather(z_ref, gz_sem.at[j], zs, me_z, peer_z))
    lax.fori_loop(done, steps, weights, 0)
    for j in range(2):
        wait_z[j]()
        part = slice(j * rhh, (j + 1) * rhh)
        rho_ref[part] = jnp.exp2(lse[part] - joined(gathered[j][1], zs) + log_cols)

    rho = rho_ref[...]
    rho_hi = rho.astype(jnp.bfloat16).astype(jnp.float32)
    rho_lo = rho - rho_hi
    zero6 = jnp.zeros((6, ys * LANES), jnp.float32)
    total = jnp.zeros((8, cols), jnp.float32)
    for z in range(zs):
        lines = []
        for part in (rho_hi, rho_lo):
            lines.append(
                jnp.concatenate([part[y * zs + z : y * zs + z + 1] for y in range(ys)], axis=1)
            )
        lhs = jnp.concatenate(lines + [zero6], axis=0).astype(jnp.bfloat16)
        total = total + jnp.dot(lhs, p_ref[z], preferred_element_type=jnp.float32)
    total = total[0:1] + total[1:2]
    for c in range(cch):
        st3_ref[me_n, c : c + 1, :] = total[:, c * LANES : (c + 1) * LANES]
    gather(st3_ref, s3_sem, n_noise, me_n, peer_noise)()
    total = st3_ref[0]
    for k in range(1, n_noise):
        total = total + st3_ref[k]
    pot_ref[...] = (epsilon * LN2) * (g1 + log_rows - jnp.log(total) * LOG2E)

    factor = float(rows * n_noise) / total
    f_hi = factor.astype(jnp.bfloat16).astype(jnp.float32)
    f_lo = factor - f_hi
    zero5 = jnp.zeros((5, LANES), jnp.float32)
    for c in range(cch):
        sl = slice(c * LANES, (c + 1) * LANES)
        tile = jnp.concatenate(
            [f_hi[c : c + 1], f_lo[c : c + 1], factor[c : c + 1], zero5], axis=0
        ).T
        d_ref[sl, 0:128] = (data_ref[sl, :].astype(jnp.float32) * tile[:, 2:3]).astype(
            jnp.bfloat16
        )
        d_ref[sl, 128:256] = jnp.zeros((LANES, 128), jnp.bfloat16)
        d_ref[sl, 128:136] = tile.astype(jnp.bfloat16)

    h = zs // 2
    offsets = [h]
    for k in range(h - 1, 0, -1):
        offsets += [k, zs - k]
    offsets.append(0)
    pending = []
    cuts = (pl.ds(0, 64), pl.ds(64, 56))
    main, last = pl.ds(0, 120), pl.ds(120, 16)

    def send(src, dst, sem, device):
        copy = pltpu.make_async_remote_copy(
            src_ref=src,
            dst_ref=dst,
            send_sem=sem.at[0],
            recv_sem=sem.at[1],
            device_id=device,
            device_id_type=MESH,
        )
        copy.start()
        pending.append(copy)

    def arrived(ref, sem):
        pltpu.make_async_copy(ref, ref, sem.at[1]).wait()

    def weigh(off):
        zt = (me_z + off) % zs
        both = jnp.dot(p_ref[zt], d_ref[...], preferred_element_type=jnp.float32)
        for y in range(ys):
            line = rho_ref[pl.ds(y * zs + zt, 1), :]
            column = jnp.broadcast_to(line, (8, LANES)).T[:, 0:1]
            part = both[y * LANES : (y + 1) * LANES] * column
            num_ref[zt, y, 0:56, :] = part[0:56, 0:128]
            num_ref[zt, y, 56:64, :] = part[:, 128:136].T
            num_ref[zt, y, 64:136, :] = part[56:128, 0:128]

    def along(way, step):
        return (me_y + (step if way == 0 else ys - step)) % ys

    def y_far(i):
        zt = (me_z + offsets[i]) % zs
        if ys == 4:
            for way in range(2):
                send(
                    num_ref.at[zt, along(way, 2), cuts[way]],
                    far_ref.at[i, cuts[way]],
                    far_sem.at[i, way],
                    peer_y(1 if way == 0 else ys - 1),
                )

    def y_near(i):
        zt = (me_z + offsets[i]) % zs
        for way in range(2):
            send(
                num_ref.at[zt, along(way, 1), cuts[1 - way]],
                near_ref.at[way, i, cuts[1 - way]],
                near_sem.at[way, i, 0],
                peer_y(1 if way == 0 else ys - 1),
            )

    def y_forward(i):
        if ys != 4:
            return
        zt = (me_z + offsets[i]) % zs
        for way in range(2):
            arrived(far_ref.at[i, cuts[way]], far_sem.at[i, way])
            to = along(way, 1)
            num_ref[zt, to, cuts[way]] = num_ref[zt, to, cuts[way]] + far_ref[i, cuts[way]]
            send(
                num_ref.at[zt, to, cuts[way]],
                near_ref.at[way, i, cuts[way]],
                near_sem.at[way, i, 1],
                peer_y(1 if way == 0 else ys - 1),
            )

    def y_merge(i):
        zt = (me_z + offsets[i]) % zs
        for way in range(2):
            arrived(near_ref.at[way, i, cuts[1 - way]], near_sem.at[way, i, 0])
            if ys == 4:
                arrived(near_ref.at[way, i, cuts[way]], near_sem.at[way, i, 1])
        if ys == 4:
            num_ref[zt, me_y, main] = num_ref[zt, me_y, main] + near_ref[0, i] + near_ref[1, i]
        else:
            for way in range(2):
                part = cuts[1 - way]
                num_ref[zt, me_y, part] = num_ref[zt, me_y, part] + near_ref[way, i, part]
        if offsets[i]:
            source = num_ref.at[zt, me_y, main]
            send(source, rz_ref.at[i], rz_sem.at[i], peer_z(offsets[i]))

    def z_first(i):
        if offsets[i]:
            source = num_ref.at[(me_z + offsets[i]) % zs, :, last]
            send(source, zf_ref.at[i], zf_sem.at[i], peer_z(offsets[i]))

    def z_merge():
        total = num_ref[me_z, :, last]
        for i in range(zs - 1):
            arrived(zf_ref.at[i], zf_sem.at[i])
            total = total + zf_ref[i]
        num_ref[me_z, :, last] = total
        for step in range(1, ys):
            source = num_ref.at[me_z, (me_y + step) % ys, last]
            send(source, yf_ref.at[step - 1], yf_sem.at[step - 1], peer_y(step))

    for i in range(zs):
        weigh(offsets[i])
        y_far(i)
        z_first(i)
    for i in range(zs):
        y_near(i)
        y_forward(i)
    z_merge()
    for i in range(zs):
        y_merge(i)
    rest = num_ref[me_z, me_y, last]
    for step in range(1, ys):
        arrived(yf_ref.at[step - 1], yf_sem.at[step - 1])
        rest = rest + yf_ref[step - 1]
    mine = num_ref[me_z, me_y, main]
    for i in range(zs - 1):
        arrived(rz_ref.at[i], rz_sem.at[i])
        mine = mine + rz_ref[i]
    den = (mine[56:64]).T
    den = den[:, 0:1] + den[:, 1:2]
    targets_ref[0:56, :] = mine[0:56] / den[0:56]
    targets_ref[56:112, :] = mine[64:120] / den[56:112]
    targets_ref[112:128, :] = rest / den[112:128]
    for copy in pending:
        copy.wait_send()


def shards(noise_latents, data_latents, projection):
    rows, width = noise_latents.shape
    cols = data_latents.shape[0]
    kdim = projection.shape[1]
    n_noise, n_dp = lax.axis_size("noise"), lax.axis_size("dp")
    ys, zs = ring_sizes(n_dp)
    rch, cch = rows // LANES, cols // LANES
    f32, bf16 = jnp.float32, jnp.bfloat16
    cfg = (rows, cols, n_noise, n_dp, kdim)
    dma = pltpu.SemaphoreType.DMA
    vmem = pl.BlockSpec(memory_space=pltpu.VMEM)
    targets, pot = pl.pallas_call(
        functools.partial(kernel, cfg),
        out_shape=(
            pltpu.VMEM((LANES, width), f32),
            pltpu.VMEM((cch, LANES), f32),
        ),
        in_specs=[vmem] * 3,
        out_specs=(vmem, vmem),
        scratch_shapes=[
            pltpu.VMEM((rows, 256), bf16),
            pltpu.VMEM((cols, 256), bf16),
            pltpu.VMEM((zs, ys * LANES, cols), bf16),
            pltpu.VMEM((cols, 256), bf16),
            pltpu.VMEM((2 * kdim, width), bf16),
            pltpu.VMEM((rch, LANES), f32),
            pltpu.VMEM((cch, LANES), f32),
            pltpu.VMEM((n_noise, cch // 2, LANES), f32),
            pltpu.VMEM((n_noise, cch // 2, LANES), f32),
            pltpu.VMEM((rch, LANES), f32),
            pltpu.VMEM((rch, LANES), f32),
            pltpu.VMEM((rch, LANES), f32),
            pltpu.VMEM((rch, LANES), f32),
            pltpu.VMEM((ys, rch // 2, LANES), f32),
            pltpu.VMEM((ys, rch // 2, LANES), f32),
            pltpu.VMEM((zs, rch // 2, LANES), f32),
            pltpu.VMEM((zs, rch // 2, LANES), f32),
            pltpu.VMEM((n_noise, cch, LANES), f32),
            pltpu.VMEM((zs, ys, 136, LANES), f32),
            pltpu.VMEM((zs, 120, LANES), f32),
            pltpu.VMEM((2, zs, 120, LANES), f32),
            pltpu.VMEM((zs - 1, 120, LANES), f32),
            pltpu.VMEM((zs - 1, ys, 16, LANES), f32),
            pltpu.VMEM((ys - 1, 16, LANES), f32),
            dma((2, 2, n_noise)),
            dma((2, n_noise)),
            dma((2, 2, ys)),
            dma((2, 2, zs)),
            dma((zs, 2, 2)),
            dma((2, zs, 2, 2)),
            dma((zs - 1, 2)),
            dma((zs - 1, 2)),
            dma((ys - 1, 2)),
        ],
        compiler_params=pltpu.CompilerParams(
            collective_id=0, has_side_effects=True, vmem_limit_bytes=56 * 2**20
        ),
        cost_estimate=pl.CostEstimate(
            flops=8 * rows * cols * 256, bytes_accessed=2**21, transcendentals=3 * rows * cols
        ),
    )(noise_latents, data_latents, projection.T)
    return (targets, pot.reshape(cols))


def solution(mesh):
    in_specs = (P("noise", None), P("dp", None), P())
    out_specs = (P(("noise", "dp"), None), P("dp"))
    return jax.shard_map(shards, mesh=mesh, in_specs=in_specs, out_specs=out_specs, check_vma=False)
```

```python
import functools
import math

import jax
import jax.numpy as jnp
from jax import lax
from jax.experimental import pallas as pl
from jax.experimental.pallas import tpu as pltpu
from jax.sharding import PartitionSpec as P

epsilon = 0.02
LOG2E = 1.0 / math.log(2.0)
LN2 = math.log(2.0)
NT = (((1,), (1,)), ((), ()))
MESH = pl.DeviceIdType.MESH
LANES = 128


def ring_sizes(dp):
    return {32: (4, 8), 8: (2, 4), 16: (4, 4)}[dp]


def split3(x):
    hi = x.astype(jnp.bfloat16).astype(jnp.float32)
    rest = x - hi
    mid = rest.astype(jnp.bfloat16).astype(jnp.float32)
    return hi, mid, rest - mid


def kernel(
    cfg,
    noise_ref,
    data_ref,
    proj_ref,
    targets_ref,
    pot_ref,
    q_ref,
    r_ref,
    p_ref,
    d_ref,
    proj2_ref,
    ul_ref,
    vl_ref,
    st1a_ref,
    st1b_ref,
    lsea_ref,
    lseb_ref,
    lse_ref,
    rho_ref,
    gya_ref,
    gyb_ref,
    gza_ref,
    gzb_ref,
    st3_ref,
    num_ref,
    far_ref,
    near_ref,
    rz_ref,
    zf_ref,
    yf_ref,
    s1_sem,
    s3_sem,
    gy_sem,
    gz_sem,
    far_sem,
    near_sem,
    rz_sem,
    zf_sem,
    yf_sem,
):
    rows, cols, n_noise, n_dp, kdim = cfg
    ys, zs = ring_sizes(n_dp)
    rch, cch = rows // LANES, cols // LANES
    log_rows = math.log2(rows * n_noise)
    log_cols = math.log2(cols * n_dp)
    scale = 2.0 * LOG2E / (kdim * epsilon)
    norm_scale = LOG2E / (kdim * epsilon)
    me_n = lax.axis_index("noise")
    me_d = lax.axis_index("dp")
    me_y, me_z = me_d // zs, me_d % zs

    def peer_noise(step):
        return ((me_n + step) % n_noise, me_d)

    def peer_y(step):
        return (me_n, (me_y + step) % ys * zs + me_z)

    def peer_z(step):
        return (me_n, me_y * zs + (me_z + step) % zs)

    barrier = pltpu.get_barrier_semaphore()

    def greet_noise(k, carry):
        pl.semaphore_signal(barrier, inc=1, device_id=peer_noise(k), device_id_type=MESH)
        return carry

    def greet_y(k, carry):
        pl.semaphore_signal(barrier, inc=1, device_id=peer_y(k), device_id_type=MESH)
        return carry

    def greet_z(k, carry):
        pl.semaphore_signal(barrier, inc=1, device_id=peer_z(k), device_id_type=MESH)
        return carry

    lax.fori_loop(1, n_noise, greet_noise, 0)
    lax.fori_loop(1, ys, greet_y, 0)
    lax.fori_loop(1, zs, greet_z, 0)

    proj2_ref[0:kdim, :] = proj_ref[...]
    proj2_ref[kdim : 2 * kdim, :] = proj_ref[...]
    half = jnp.full((8, LANES), 0.5, jnp.bfloat16)
    one = jnp.ones((1, LANES), jnp.float32)
    zero = jnp.zeros((2, LANES), jnp.float32)

    def put_bias(dst_ref, c, bias, first):
        parts = list(split3(bias))
        ones = [one, one, one]
        tile = jnp.concatenate((parts + ones if first else ones + parts) + [zero], axis=0)
        dst_ref[c * LANES : (c + 1) * LANES, 128:136] = tile.T.astype(jnp.bfloat16)

    def prepare(src_ref, dst_ref, bias_ref, count, is_q):
        step = min(2048, count)

        def body(b, carry):
            sl = pl.ds(pl.multiple_of(b * step, step), step)
            proj = lax.dot_general(
                src_ref[sl, :], proj2_ref[...], NT, preferred_element_type=jnp.float32
            )
            code = proj.astype(jnp.bfloat16)
            full = code.astype(jnp.float32)
            square = full * full
            sq_hi = square.astype(jnp.bfloat16)
            sq_lo = (square - sq_hi.astype(jnp.float32)).astype(jnp.bfloat16)
            norm = lax.dot_general(
                half, sq_hi, NT, preferred_element_type=jnp.float32
            ) + lax.dot_general(half, sq_lo, NT, preferred_element_type=jnp.float32)
            if is_q:
                dst_ref[sl, 0:128] = code
            else:
                scaled = full * scale
                hi = scaled.astype(jnp.bfloat16)
                lo = (scaled - hi.astype(jnp.float32)).astype(jnp.bfloat16)
                lane = lax.broadcasted_iota(jnp.int32, scaled.shape, 1)
                dst_ref[sl, 0:128] = jnp.where(
                    lane < kdim, hi.astype(jnp.float32), lo.astype(jnp.float32)
                ).astype(jnp.bfloat16)
            dst_ref[sl, 128:256] = jnp.zeros((step, 128), jnp.bfloat16)
            for c in range(step // LANES):
                bias_ref[pl.ds(b * (step // LANES) + c, 1), :] = (
                    -norm_scale * norm[0:1, c * LANES : (c + 1) * LANES]
                )
            return carry

        lax.fori_loop(0, count // step, body, 0)
        bias = bias_ref[...]
        for c in range(count // LANES):
            put_bias(dst_ref, c, bias[c : c + 1, :], is_q)

    prepare(noise_ref, q_ref, ul_ref, rows, True)
    prepare(data_ref, r_ref, vl_ref, cols, False)

    def lse_pass(lhs_ref, first, count, rhs_ref, start, width, write):
        bw = min(2048, width)
        bl = 256
        un = max(1, min(2**21 // (bl * bw), count // bl))

        def wide(w, carry):
            rhs = rhs_ref[pl.ds(pl.multiple_of(start + w * bw, bw), bw), :]

            def body(step, state):
                top, total = state
                for u in range(un):
                    sl = pl.ds(pl.multiple_of(first + (step * un + u) * bl, bl), bl)
                    z = lax.dot_general(
                        lhs_ref[sl, :], rhs, NT, preferred_element_type=jnp.float32
                    ).reshape(bl // 8, 8, bw)
                    new = jnp.maximum(top, jnp.max(z, axis=0))
                    total = total * jnp.exp2(top - new) + jnp.sum(jnp.exp2(z - new[None]), axis=0)
                    top = new
                return top, total

            state = (jnp.full((8, bw), -1e30, jnp.float32), jnp.zeros((8, bw), jnp.float32))
            top, total = lax.fori_loop(0, count // (bl * un), body, state)
            best = jnp.max(top, axis=0, keepdims=True)
            total = jnp.sum(total * jnp.exp2(top - best), axis=0, keepdims=True)
            lse = best + jnp.log(total) * LOG2E
            for c in range(bw // LANES):
                write(w * (bw // LANES) + c, lse[:, c * LANES : (c + 1) * LANES])
            return carry

        lax.fori_loop(0, width // bw, wide, 0)

    def gather(ref, sem, size, me, peer):
        def copy(k):
            return pltpu.make_async_remote_copy(
                src_ref=ref.at[me],
                dst_ref=ref.at[me],
                send_sem=sem.at[0, k],
                recv_sem=sem.at[1, me],
                device_id=peer(k),
                device_id_type=MESH,
            )

        def start(k, carry):
            copy(k).start()
            return carry

        def wait(k, carry):
            source = (me + size - k) % size
            pltpu.make_async_copy(ref.at[source], ref.at[source], sem.at[1, source]).wait()
            copy(k).wait_send()
            return carry

        lax.fori_loop(1, size, start, 0)
        return lambda: lax.fori_loop(1, size, wait, 0)

    def joined(ref, size):
        top = ref[0]
        for k in range(1, size):
            top = jnp.maximum(top, ref[k])
        total = jnp.exp2(ref[0] - top)
        for k in range(1, size):
            total = total + jnp.exp2(ref[k] - top)
        return top + jnp.log(total) * LOG2E

    hcol, hch = cols // 2, cch // 2
    waits, g1 = [], []
    for i, ref in enumerate((st1a_ref, st1b_ref)):

        def write(chunk, line):
            ref[me_n, pl.ds(chunk, 1), :] = line

        lse_pass(q_ref, 0, rows, r_ref, i * hcol, hcol, write)
        if i == 0:
            pl.semaphore_wait(barrier, n_noise - 1 + ys - 1 + zs - 1)
        waits.append(gather(ref, s1_sem.at[i], n_noise, me_n, peer_noise))
    hrow, rhh = rows // 2, rch // 2
    wait_y, gathered = [], ((gya_ref, gza_ref), (gyb_ref, gzb_ref))
    for i, (ref, out_ref) in enumerate(((st1a_ref, lsea_ref), (st1b_ref, lseb_ref))):
        waits[i]()
        g1.append(log_rows - joined(ref, n_noise))
        vl = vl_ref[i * hch : (i + 1) * hch] + g1[i]
        for c in range(hch):
            put_bias(r_ref, i * hch + c, vl[c : c + 1, :], False)

        def write(chunk, line):
            out_ref[pl.ds(chunk, 1), :] = line

        if i == 0:
            lse_pass(r_ref, 0, hcol, q_ref, 0, rows, write)
            continue
        for j in range(2):
            lse_pass(
                r_ref, hcol, hcol, q_ref, j * hrow, hrow, lambda c, x: write(j * rhh + c, x)
            )
            part = slice(j * rhh, (j + 1) * rhh)
            one_half, other = lsea_ref[part], lseb_ref[part]
            top = jnp.maximum(one_half, other)
            total = jnp.exp2(one_half - top) + jnp.exp2(other - top)
            lse_ref[part] = top + LOG2E * jnp.log(total)
            gathered[j][0][me_y] = lse_ref[part]
            wait_y.append(gather(gathered[j][0], gy_sem.at[j], ys, me_y, peer_y))
    g1 = jnp.concatenate(g1, axis=0)

    bl, bw, un = 256, cols, min(4, rows // 256)
    per = bl // LANES

    def weights(step, carry):
        for u in range(un):
            tile = step * un + u
            sl = pl.ds(pl.multiple_of(tile * bl, bl), bl)
            z = lax.dot_general(q_ref[sl, :], r_ref[...], NT, preferred_element_type=jnp.float32)
            p = jnp.exp2(z).astype(jnp.bfloat16)
            for i in range(per):
                chunk = tile * per + i
                put = pl.ds(pl.multiple_of(chunk // zs * LANES, LANES), LANES)
                p_ref[chunk % zs, put, :] = p[i * LANES : (i + 1) * LANES]
        return carry

    steps = rows // (bl * un)
    lse = lse_ref[...]
    ul = ul_ref[...] - lse
    for c in range(rch):
        put_bias(q_ref, c, ul[c : c + 1, :], True)
    wait_z = []
    done = 0
    for j, (y_ref, z_ref) in enumerate(gathered):
        upto = steps * (j + 1) // 4
        lax.fori_loop(done, upto, weights, 0)
        done = upto
        wait_y[j]()
        z_ref[me_z] = joined(y_ref, ys)
        wait_z.append(gather(z_ref, gz_sem.at[j], zs, me_z, peer_z))
    lax.fori_loop(done, steps, weights, 0)
    hys = ys // 2
    zero6 = jnp.zeros((6, hys * LANES), jnp.float32)
    total = jnp.zeros((8, cols), jnp.float32)
    for j in range(2):
        wait_z[j]()
        part = slice(j * rhh, (j + 1) * rhh)
        rho = jnp.exp2(lse[part] - joined(gathered[j][1], zs) + log_cols)
        rho_ref[part] = rho
        rho_hi = rho.astype(jnp.bfloat16).astype(jnp.float32)
        rho_lo = rho - rho_hi
        for z in range(zs):
            lines = []
            for half_rho in (rho_hi, rho_lo):
                lines.append(
                    jnp.concatenate(
                        [half_rho[y * zs + z : y * zs + z + 1] for y in range(hys)], axis=1
                    )
                )
            lhs = jnp.concatenate(lines + [zero6], axis=0).astype(jnp.bfloat16)
            block = p_ref[z, j * hys * LANES : (j + 1) * hys * LANES]
            total = total + jnp.dot(lhs, block, preferred_element_type=jnp.float32)
    total = total[0:1] + total[1:2]
    for c in range(cch):
        st3_ref[me_n, c : c + 1, :] = total[:, c * LANES : (c + 1) * LANES]
    gather(st3_ref, s3_sem, n_noise, me_n, peer_noise)()
    total = st3_ref[0]
    for k in range(1, n_noise):
        total = total + st3_ref[k]

    factor = float(rows * n_noise) / total
    f_hi = factor.astype(jnp.bfloat16).astype(jnp.float32)
    f_lo = factor - f_hi
    zero5 = jnp.zeros((5, LANES), jnp.float32)
    for c in range(cch):
        sl = slice(c * LANES, (c + 1) * LANES)
        tile = jnp.concatenate(
            [f_hi[c : c + 1], f_lo[c : c + 1], factor[c : c + 1], zero5], axis=0
        ).T
        d_ref[sl, 0:128] = (data_ref[sl, :].astype(jnp.float32) * tile[:, 2:3]).astype(
            jnp.bfloat16
        )
        d_ref[sl, 128:256] = jnp.zeros((LANES, 128), jnp.bfloat16)
        d_ref[sl, 128:136] = tile.astype(jnp.bfloat16)

    h = zs // 2
    offsets = [h]
    for k in range(h - 1, 0, -1):
        offsets += [k, zs - k]
    offsets.append(0)
    pending = []
    cuts = (pl.ds(0, 56), pl.ds(56, 56))
    main, last = pl.ds(0, 112), pl.ds(112, 24)

    def send(src, dst, sem, device):
        copy = pltpu.make_async_remote_copy(
            src_ref=src,
            dst_ref=dst,
            send_sem=sem.at[0],
            recv_sem=sem.at[1],
            device_id=device,
            device_id_type=MESH,
        )
        copy.start()
        pending.append(copy)

    def arrived(ref, sem):
        pltpu.make_async_copy(ref, ref, sem.at[1]).wait()

    def weigh(off):
        zt = (me_z + off) % zs
        both = jnp.dot(p_ref[zt], d_ref[...], preferred_element_type=jnp.float32)
        for y in range(ys):
            line = rho_ref[pl.ds(y * zs + zt, 1), :]
            column = jnp.broadcast_to(line, (8, LANES)).T[:, 0:1]
            part = both[y * LANES : (y + 1) * LANES] * column
            num_ref[zt, y, 0:48, :] = part[0:48, 0:128]
            num_ref[zt, y, 48:56, :] = part[:, 128:136].T
            num_ref[zt, y, 56:136, :] = part[48:128, 0:128]

    def along(way, step):
        return (me_y + (step if way == 0 else ys - step)) % ys

    def y_far(i):
        zt = (me_z + offsets[i]) % zs
        if ys == 4:
            for way in range(2):
                send(
                    num_ref.at[zt, along(way, 2), cuts[way]],
                    far_ref.at[i, cuts[way]],
                    far_sem.at[i, way],
                    peer_y(1 if way == 0 else ys - 1),
                )

    def y_near(i):
        zt = (me_z + offsets[i]) % zs
        for way in range(2):
            send(
                num_ref.at[zt, along(way, 1), cuts[1 - way]],
                near_ref.at[way, i, cuts[1 - way]],
                near_sem.at[way, i, 0],
                peer_y(1 if way == 0 else ys - 1),
            )

    def y_forward(i):
        if ys != 4:
            return
        zt = (me_z + offsets[i]) % zs
        for way in range(2):
            arrived(far_ref.at[i, cuts[way]], far_sem.at[i, way])
            to = along(way, 1)
            num_ref[zt, to, cuts[way]] = num_ref[zt, to, cuts[way]] + far_ref[i, cuts[way]]
            send(
                num_ref.at[zt, to, cuts[way]],
                near_ref.at[way, i, cuts[way]],
                near_sem.at[way, i, 1],
                peer_y(1 if way == 0 else ys - 1),
            )

    def y_merge(i):
        zt = (me_z + offsets[i]) % zs
        for way in range(2):
            arrived(near_ref.at[way, i, cuts[1 - way]], near_sem.at[way, i, 0])
            if ys == 4:
                arrived(near_ref.at[way, i, cuts[way]], near_sem.at[way, i, 1])
        if ys == 4:
            num_ref[zt, me_y, main] = num_ref[zt, me_y, main] + near_ref[0, i] + near_ref[1, i]
        else:
            for way in range(2):
                part = cuts[1 - way]
                num_ref[zt, me_y, part] = num_ref[zt, me_y, part] + near_ref[way, i, part]
        if offsets[i]:
            source = num_ref.at[zt, me_y, main]
            send(source, rz_ref.at[i], rz_sem.at[i], peer_z(offsets[i]))

    def z_first(i):
        if offsets[i]:
            source = num_ref.at[(me_z + offsets[i]) % zs, :, last]
            send(source, zf_ref.at[i], zf_sem.at[i], peer_z(offsets[i]))

    def z_merge():
        total = num_ref[me_z, :, last]
        for i in range(zs - 1):
            arrived(zf_ref.at[i], zf_sem.at[i])
            total = total + zf_ref[i]
        num_ref[me_z, :, last] = total
        for step in range(1, ys):
            source = num_ref.at[me_z, (me_y + step) % ys, last]
            send(source, yf_ref.at[step - 1], yf_sem.at[step - 1], peer_y(step))

    for i in range(zs):
        weigh(offsets[i])
        y_far(i)
        z_first(i)
    for i in range(zs):
        y_near(i)
        y_forward(i)
    pot_ref[...] = (epsilon * LN2) * (g1 + log_rows - jnp.log(total) * LOG2E)
    for i in range(zs):
        if i == zs // 2:
            z_merge()
        y_merge(i)
    for copy in pending:
        copy.wait_send()
    rest = num_ref[me_z, me_y, last]
    for step in range(1, ys):
        arrived(yf_ref.at[step - 1], yf_sem.at[step - 1])
        rest = rest + yf_ref[step - 1]
    mine = num_ref[me_z, me_y, main]
    for i in range(zs - 1):
        arrived(rz_ref.at[i], rz_sem.at[i])
        mine = mine + rz_ref[i]
    den = (mine[48:56]).T
    den = den[:, 0:1] + den[:, 1:2]
    targets_ref[0:48, :] = mine[0:48] / den[0:48]
    targets_ref[48:104, :] = mine[56:112] / den[48:104]
    targets_ref[104:128, :] = rest / den[104:128]


def shards(noise_latents, data_latents, projection):
    rows, width = noise_latents.shape
    cols = data_latents.shape[0]
    kdim = projection.shape[1]
    n_noise, n_dp = lax.axis_size("noise"), lax.axis_size("dp")
    ys, zs = ring_sizes(n_dp)
    rch, cch = rows // LANES, cols // LANES
    f32, bf16 = jnp.float32, jnp.bfloat16
    cfg = (rows, cols, n_noise, n_dp, kdim)
    dma = pltpu.SemaphoreType.DMA
    vmem = pl.BlockSpec(memory_space=pltpu.VMEM)
    targets, pot = pl.pallas_call(
        functools.partial(kernel, cfg),
        out_shape=(
            pltpu.VMEM((LANES, width), f32),
            pltpu.VMEM((cch, LANES), f32),
        ),
        in_specs=[vmem] * 3,
        out_specs=(vmem, vmem),
        scratch_shapes=[
            pltpu.VMEM((rows, 256), bf16),
            pltpu.VMEM((cols, 256), bf16),
            pltpu.VMEM((zs, ys * LANES, cols), bf16),
            pltpu.VMEM((cols, 256), bf16),
            pltpu.VMEM((2 * kdim, width), bf16),
            pltpu.VMEM((rch, LANES), f32),
            pltpu.VMEM((cch, LANES), f32),
            pltpu.VMEM((n_noise, cch // 2, LANES), f32),
            pltpu.VMEM((n_noise, cch // 2, LANES), f32),
            pltpu.VMEM((rch, LANES), f32),
            pltpu.VMEM((rch, LANES), f32),
            pltpu.VMEM((rch, LANES), f32),
            pltpu.VMEM((rch, LANES), f32),
            pltpu.VMEM((ys, rch // 2, LANES), f32),
            pltpu.VMEM((ys, rch // 2, LANES), f32),
            pltpu.VMEM((zs, rch // 2, LANES), f32),
            pltpu.VMEM((zs, rch // 2, LANES), f32),
            pltpu.VMEM((n_noise, cch, LANES), f32),
            pltpu.VMEM((zs, ys, 136, LANES), f32),
            pltpu.VMEM((zs, 112, LANES), f32),
            pltpu.VMEM((2, zs, 112, LANES), f32),
            pltpu.VMEM((zs - 1, 112, LANES), f32),
            pltpu.VMEM((zs - 1, ys, 24, LANES), f32),
            pltpu.VMEM((ys - 1, 24, LANES), f32),
            dma((2, 2, n_noise)),
            dma((2, n_noise)),
            dma((2, 2, ys)),
            dma((2, 2, zs)),
            dma((zs, 2, 2)),
            dma((2, zs, 2, 2)),
            dma((zs - 1, 2)),
            dma((zs - 1, 2)),
            dma((ys - 1, 2)),
        ],
        compiler_params=pltpu.CompilerParams(
            collective_id=0, has_side_effects=True, vmem_limit_bytes=56 * 2**20
        ),
        cost_estimate=pl.CostEstimate(
            flops=8 * rows * cols * 256, bytes_accessed=2**21, transcendentals=3 * rows * cols
        ),
    )(noise_latents, data_latents, projection.T)
    return (targets, pot.reshape(cols))


def solution(mesh):
    in_specs = (P("noise", None), P("dp", None), P())
    out_specs = (P(("noise", "dp"), None), P("dp"))
    return jax.shard_map(shards, mesh=mesh, in_specs=in_specs, out_specs=out_specs, check_vma=False)
```

```python
import functools
import math

import jax
import jax.numpy as jnp
from jax import lax
from jax.experimental import pallas as pl
from jax.experimental.pallas import tpu as pltpu
from jax.sharding import PartitionSpec as P

epsilon = 0.02
LOG2E = 1.0 / math.log(2.0)
LN2 = math.log(2.0)
NT = (((1,), (1,)), ((), ()))
MESH = pl.DeviceIdType.MESH
LANES = 128


def ring_sizes(dp):
    return {32: (4, 8), 8: (2, 4), 16: (4, 4)}[dp]


def split3(x):
    hi = x.astype(jnp.bfloat16).astype(jnp.float32)
    rest = x - hi
    mid = rest.astype(jnp.bfloat16).astype(jnp.float32)
    return hi, mid, rest - mid


def kernel(
    cfg,
    noise_in,
    data_in,
    proj_in,
    targets_ref,
    pot_ref,
    noise_ref,
    data_ref,
    proj_ref,
    q_ref,
    r_ref,
    p_ref,
    d_ref,
    proj2_ref,
    ul_ref,
    vl_ref,
    st1a_ref,
    st1b_ref,
    lsea_ref,
    lseb_ref,
    lse_ref,
    rho_ref,
    gya_ref,
    gyb_ref,
    gza_ref,
    gzb_ref,
    st3_ref,
    num_ref,
    far_ref,
    near_ref,
    rz_ref,
    zf_ref,
    yf_ref,
    den_ref,
    dy_ref,
    dz_ref,
    s1_sem,
    s3_sem,
    gy_sem,
    gz_sem,
    far_sem,
    near_sem,
    rz_sem,
    zf_sem,
    yf_sem,
    dy_sem,
    dz_sem,
    in_sem,
):
    rows, cols, n_noise, n_dp, kdim = cfg
    ys, zs = ring_sizes(n_dp)
    rch, cch = rows // LANES, cols // LANES
    log_rows = math.log2(rows * n_noise)
    log_cols = math.log2(cols * n_dp)
    scale = 2.0 * LOG2E / (kdim * epsilon)
    norm_scale = LOG2E / (kdim * epsilon)
    me_n = lax.axis_index("noise")
    me_d = lax.axis_index("dp")
    me_y, me_z = me_d // zs, me_d % zs

    def peer_noise(step):
        return ((me_n + step) % n_noise, me_d)

    def peer_y(step):
        return (me_n, (me_y + step) % ys * zs + me_z)

    def peer_z(step):
        return (me_n, me_y * zs + (me_z + step) % zs)

    hrow = rows // 2
    loads = [
        pltpu.make_async_copy(src, dst, in_sem.at[i])
        for i, (src, dst) in enumerate(
            (
                (proj_in, proj_ref),
                (data_in, data_ref),
                (noise_in.at[0:hrow], noise_ref.at[0:hrow]),
                (noise_in.at[hrow:rows], noise_ref.at[hrow:rows]),
            )
        )
    ]
    for load in loads:
        load.start()
    barrier = pltpu.get_barrier_semaphore()

    def greet_noise(k, carry):
        pl.semaphore_signal(barrier, inc=1, device_id=peer_noise(k), device_id_type=MESH)
        return carry

    def greet_y(k, carry):
        pl.semaphore_signal(barrier, inc=1, device_id=peer_y(k), device_id_type=MESH)
        return carry

    def greet_z(k, carry):
        pl.semaphore_signal(barrier, inc=1, device_id=peer_z(k), device_id_type=MESH)
        return carry

    lax.fori_loop(1, n_noise, greet_noise, 0)
    lax.fori_loop(1, ys, greet_y, 0)
    lax.fori_loop(1, zs, greet_z, 0)

    loads[0].wait()
    proj2_ref[0:kdim, :] = proj_ref[...]
    proj2_ref[kdim : 2 * kdim, :] = proj_ref[...]
    half = jnp.full((8, LANES), 0.5, jnp.bfloat16)
    one = jnp.ones((1, LANES), jnp.float32)
    zero = jnp.zeros((2, LANES), jnp.float32)

    def put_bias(dst_ref, c, bias, first):
        parts = list(split3(bias))
        ones = [one, one, one]
        tile = jnp.concatenate((parts + ones if first else ones + parts) + [zero], axis=0)
        dst_ref[c * LANES : (c + 1) * LANES, 128:136] = tile.T.astype(jnp.bfloat16)

    def prepare(src_ref, dst_ref, bias_ref, count, is_q, parts):
        step = count // len(parts)
        for b, load in enumerate(parts):
            load.wait()
            sl = pl.ds(b * step, step)
            proj = lax.dot_general(
                src_ref[sl, :], proj2_ref[...], NT, preferred_element_type=jnp.float32
            )
            code = proj.astype(jnp.bfloat16)
            full = code.astype(jnp.float32)
            square = full * full
            sq_hi = square.astype(jnp.bfloat16)
            sq_lo = (square - sq_hi.astype(jnp.float32)).astype(jnp.bfloat16)
            norm = lax.dot_general(
                half, sq_hi, NT, preferred_element_type=jnp.float32
            ) + lax.dot_general(half, sq_lo, NT, preferred_element_type=jnp.float32)
            if is_q:
                dst_ref[sl, 0:128] = code
            else:
                scaled = full * scale
                hi = scaled.astype(jnp.bfloat16)
                lo = (scaled - hi.astype(jnp.float32)).astype(jnp.bfloat16)
                lane = lax.broadcasted_iota(jnp.int32, scaled.shape, 1)
                dst_ref[sl, 0:128] = jnp.where(
                    lane < kdim, hi.astype(jnp.float32), lo.astype(jnp.float32)
                ).astype(jnp.bfloat16)
            dst_ref[sl, 128:256] = jnp.zeros((step, 128), jnp.bfloat16)
            for c in range(step // LANES):
                bias_ref[pl.ds(b * (step // LANES) + c, 1), :] = (
                    -norm_scale * norm[0:1, c * LANES : (c + 1) * LANES]
                )
        bias = bias_ref[...]
        for c in range(count // LANES):
            put_bias(dst_ref, c, bias[c : c + 1, :], is_q)

    prepare(data_ref, r_ref, vl_ref, cols, False, loads[1:2])
    prepare(noise_ref, q_ref, ul_ref, rows, True, loads[2:4])

    def lse_pass(lhs_ref, first, count, rhs_ref, start, width, write):
        bw = min(2048, width)
        bl = 256
        un = max(1, min(2**21 // (bl * bw), count // bl))

        def wide(w, carry):
            rhs = rhs_ref[pl.ds(pl.multiple_of(start + w * bw, bw), bw), :]

            def body(step, state):
                top, total = state
                for u in range(un):
                    sl = pl.ds(pl.multiple_of(first + (step * un + u) * bl, bl), bl)
                    z = lax.dot_general(
                        lhs_ref[sl, :], rhs, NT, preferred_element_type=jnp.float32
                    ).reshape(bl // 8, 8, bw)
                    new = jnp.maximum(top, jnp.max(z, axis=0))
                    total = total * jnp.exp2(top - new) + jnp.sum(jnp.exp2(z - new[None]), axis=0)
                    top = new
                return top, total

            state = (jnp.full((8, bw), -1e30, jnp.float32), jnp.zeros((8, bw), jnp.float32))
            top, total = lax.fori_loop(0, count // (bl * un), body, state)
            best = jnp.max(top, axis=0, keepdims=True)
            total = jnp.sum(total * jnp.exp2(top - best), axis=0, keepdims=True)
            lse = best + jnp.log(total) * LOG2E
            for c in range(bw // LANES):
                write(w * (bw // LANES) + c, lse[:, c * LANES : (c + 1) * LANES])
            return carry

        lax.fori_loop(0, width // bw, wide, 0)

    def gather(ref, sem, size, me, peer):
        def copy(k):
            return pltpu.make_async_remote_copy(
                src_ref=ref.at[me],
                dst_ref=ref.at[me],
                send_sem=sem.at[0, k],
                recv_sem=sem.at[1, me],
                device_id=peer(k),
                device_id_type=MESH,
            )

        def start(k, carry):
            copy(k).start()
            return carry

        def wait(k, carry):
            source = (me + size - k) % size
            pltpu.make_async_copy(ref.at[source], ref.at[source], sem.at[1, source]).wait()
            copy(k).wait_send()
            return carry

        lax.fori_loop(1, size, start, 0)
        return lambda: lax.fori_loop(1, size, wait, 0)

    def joined(ref, size):
        top = ref[0]
        for k in range(1, size):
            top = jnp.maximum(top, ref[k])
        total = jnp.exp2(ref[0] - top)
        for k in range(1, size):
            total = total + jnp.exp2(ref[k] - top)
        return top + jnp.log(total) * LOG2E

    hcol, hch = cols // 2, cch // 2
    waits, g1 = [], []
    for i, ref in enumerate((st1a_ref, st1b_ref)):

        def write(chunk, line):
            ref[me_n, pl.ds(chunk, 1), :] = line

        lse_pass(q_ref, 0, rows, r_ref, i * hcol, hcol, write)
        if i == 0:
            pl.semaphore_wait(barrier, n_noise - 1 + ys - 1 + zs - 1)
        waits.append(gather(ref, s1_sem.at[i], n_noise, me_n, peer_noise))
    rhh = rch // 2
    wait_y, gathered = [], ((gya_ref, gza_ref), (gyb_ref, gzb_ref))
    for i, (ref, out_ref) in enumerate(((st1a_ref, lsea_ref), (st1b_ref, lseb_ref))):
        waits[i]()
        g1.append(log_rows - joined(ref, n_noise))
        vl = vl_ref[i * hch : (i + 1) * hch] + g1[i]
        for c in range(hch):
            put_bias(r_ref, i * hch + c, vl[c : c + 1, :], False)

        def write(chunk, line):
            out_ref[pl.ds(chunk, 1), :] = line

        if i == 0:
            lse_pass(r_ref, 0, hcol, q_ref, 0, rows, write)
            continue
        for j in range(2):
            lse_pass(
                r_ref, hcol, hcol, q_ref, j * hrow, hrow, lambda c, x: write(j * rhh + c, x)
            )
            part = slice(j * rhh, (j + 1) * rhh)
            one_half, other = lsea_ref[part], lseb_ref[part]
            top = jnp.maximum(one_half, other)
            total = jnp.exp2(one_half - top) + jnp.exp2(other - top)
            lse_ref[part] = top + LOG2E * jnp.log(total)
            gathered[j][0][me_y] = lse_ref[part]
            wait_y.append(gather(gathered[j][0], gy_sem.at[j], ys, me_y, peer_y))
    g1 = jnp.concatenate(g1, axis=0)

    bl, bw, un = 256, cols, min(4, rows // 256)
    per = bl // LANES

    def weights(step, carry):
        for u in range(un):
            tile = step * un + u
            sl = pl.ds(pl.multiple_of(tile * bl, bl), bl)
            z = lax.dot_general(q_ref[sl, :], r_ref[...], NT, preferred_element_type=jnp.float32)
            p = jnp.exp2(z).astype(jnp.bfloat16)
            for i in range(per):
                chunk = tile * per + i
                put = pl.ds(pl.multiple_of(chunk // zs * LANES, LANES), LANES)
                p_ref[chunk % zs, put, :] = p[i * LANES : (i + 1) * LANES]
        return carry

    steps = rows // (bl * un)
    lse = lse_ref[...]
    ul = ul_ref[...] - lse
    for c in range(rch):
        put_bias(q_ref, c, ul[c : c + 1, :], True)
    wait_z = []
    done = 0
    for j, (y_ref, z_ref) in enumerate(gathered):
        upto = steps * (j + 1) // 4
        lax.fori_loop(done, upto, weights, 0)
        done = upto
        wait_y[j]()
        z_ref[me_z] = joined(y_ref, ys)
        wait_z.append(gather(z_ref, gz_sem.at[j], zs, me_z, peer_z))
    lax.fori_loop(done, steps, weights, 0)
    hys = ys // 2
    zero6 = jnp.zeros((6, hys * LANES), jnp.float32)
    total = jnp.zeros((8, cols), jnp.float32)
    for j in range(2):
        wait_z[j]()
        part = slice(j * rhh, (j + 1) * rhh)
        rho = jnp.exp2(lse[part] - joined(gathered[j][1], zs) + log_cols)
        rho_ref[part] = rho
        rho_hi = rho.astype(jnp.bfloat16).astype(jnp.float32)
        rho_lo = rho - rho_hi
        for z in range(zs):
            lines = []
            for half_rho in (rho_hi, rho_lo):
                lines.append(
                    jnp.concatenate(
                        [half_rho[y * zs + z : y * zs + z + 1] for y in range(hys)], axis=1
                    )
                )
            lhs = jnp.concatenate(lines + [zero6], axis=0).astype(jnp.bfloat16)
            block = p_ref[z, j * hys * LANES : (j + 1) * hys * LANES]
            total = total + jnp.dot(lhs, block, preferred_element_type=jnp.float32)
    total = total[0:1] + total[1:2]
    for c in range(cch):
        st3_ref[me_n, c : c + 1, :] = total[:, c * LANES : (c + 1) * LANES]
    gather(st3_ref, s3_sem, n_noise, me_n, peer_noise)()
    total = st3_ref[0]
    for k in range(1, n_noise):
        total = total + st3_ref[k]

    factor = float(rows * n_noise) / total
    f_hi = factor.astype(jnp.bfloat16).astype(jnp.float32)
    f_lo = factor - f_hi
    zero5 = jnp.zeros((5, LANES), jnp.float32)
    for c in range(cch):
        sl = slice(c * LANES, (c + 1) * LANES)
        tile = jnp.concatenate(
            [f_hi[c : c + 1], f_lo[c : c + 1], factor[c : c + 1], zero5], axis=0
        ).T
        d_ref[sl, 0:128] = (data_ref[sl, :].astype(jnp.float32) * tile[:, 2:3]).astype(
            jnp.bfloat16
        )
        d_ref[sl, 128:256] = jnp.zeros((LANES, 128), jnp.bfloat16)
        d_ref[sl, 128:136] = tile.astype(jnp.bfloat16)

    h = zs // 2
    offsets = [h]
    for k in range(h - 1, 0, -1):
        offsets += [k, zs - k]
    offsets.append(0)
    pending = []
    cuts = (pl.ds(0, 56), pl.ds(56, 48))
    main, last = pl.ds(0, 104), pl.ds(104, 24)

    def send(src, dst, sem, device):
        copy = pltpu.make_async_remote_copy(
            src_ref=src,
            dst_ref=dst,
            send_sem=sem.at[0],
            recv_sem=sem.at[1],
            device_id=device,
            device_id_type=MESH,
        )
        copy.start()
        pending.append(copy)

    def arrived(ref, sem):
        pltpu.make_async_copy(ref, ref, sem.at[1]).wait()

    def weigh(off):
        zt = (me_z + off) % zs
        both = jnp.dot(p_ref[zt], d_ref[...], preferred_element_type=jnp.float32)
        for y in range(ys):
            line = rho_ref[pl.ds(y * zs + zt, 1), :]
            column = jnp.broadcast_to(line, (8, LANES)).T[:, 0:1]
            part = both[y * LANES : (y + 1) * LANES] * column
            num_ref[zt, y] = part[:, 0:128]
            sums = part[:, 128:136].T
            den_ref[y, zt] = sums[0:1] + sums[1:2]

    def along(way, step):
        return (me_y + (step if way == 0 else ys - step)) % ys

    def y_far(i):
        zt = (me_z + offsets[i]) % zs
        if ys == 4:
            for way in range(2):
                send(
                    num_ref.at[zt, along(way, 2), cuts[way]],
                    far_ref.at[i, cuts[way]],
                    far_sem.at[i, way],
                    peer_y(1 if way == 0 else ys - 1),
                )

    def y_near(i):
        zt = (me_z + offsets[i]) % zs
        for way in range(2):
            send(
                num_ref.at[zt, along(way, 1), cuts[1 - way]],
                near_ref.at[way, i, cuts[1 - way]],
                near_sem.at[way, i, 0],
                peer_y(1 if way == 0 else ys - 1),
            )

    def y_forward(i):
        if ys != 4:
            return
        zt = (me_z + offsets[i]) % zs
        for way in range(2):
            arrived(far_ref.at[i, cuts[way]], far_sem.at[i, way])
            to = along(way, 1)
            num_ref[zt, to, cuts[way]] = num_ref[zt, to, cuts[way]] + far_ref[i, cuts[way]]
            send(
                num_ref.at[zt, to, cuts[way]],
                near_ref.at[way, i, cuts[way]],
                near_sem.at[way, i, 1],
                peer_y(1 if way == 0 else ys - 1),
            )

    def y_merge(i):
        zt = (me_z + offsets[i]) % zs
        for way in range(2):
            arrived(near_ref.at[way, i, cuts[1 - way]], near_sem.at[way, i, 0])
            if ys == 4:
                arrived(near_ref.at[way, i, cuts[way]], near_sem.at[way, i, 1])
        if ys == 4:
            num_ref[zt, me_y, main] = num_ref[zt, me_y, main] + near_ref[0, i] + near_ref[1, i]
        else:
            for way in range(2):
                part = cuts[1 - way]
                num_ref[zt, me_y, part] = num_ref[zt, me_y, part] + near_ref[way, i, part]
        if offsets[i]:
            source = num_ref.at[zt, me_y, main]
            send(source, rz_ref.at[i], rz_sem.at[i], peer_z(offsets[i]))

    def z_first(i):
        if offsets[i]:
            source = num_ref.at[(me_z + offsets[i]) % zs, :, last]
            send(source, zf_ref.at[i], zf_sem.at[i], peer_z(offsets[i]))

    def den_first():
        for step in range(1, ys):
            source = den_ref.at[(me_y + step) % ys]
            send(source, dy_ref.at[step - 1], dy_sem.at[step - 1], peer_y(step))

    def den_merge():
        total = den_ref[me_y]
        for step in range(1, ys):
            arrived(dy_ref.at[step - 1], dy_sem.at[step - 1])
            total = total + dy_ref[step - 1]
        den_ref[me_y] = total
        for i in range(zs - 1):
            source = den_ref.at[me_y, (me_z + offsets[i]) % zs]
            send(source, dz_ref.at[i], dz_sem.at[i], peer_z(offsets[i]))

    def z_merge():
        total = num_ref[me_z, :, last]
        for i in range(zs - 1):
            arrived(zf_ref.at[i], zf_sem.at[i])
            total = total + zf_ref[i]
        num_ref[me_z, :, last] = total
        for step in range(1, ys):
            source = num_ref.at[me_z, (me_y + step) % ys, last]
            send(source, yf_ref.at[step - 1], yf_sem.at[step - 1], peer_y(step))

    for i in range(zs):
        weigh(offsets[i])
        y_far(i)
        z_first(i)
    den_first()
    for i in range(zs):
        y_near(i)
        y_forward(i)
    den_merge()
    pot_ref[...] = (epsilon * LN2) * (g1 + log_rows - jnp.log(total) * LOG2E)
    for i in range(zs):
        if i == zs // 2:
            z_merge()
        y_merge(i)
    for copy in pending:
        copy.wait_send()
    rest = num_ref[me_z, me_y, last]
    for step in range(1, ys):
        arrived(yf_ref.at[step - 1], yf_sem.at[step - 1])
        rest = rest + yf_ref[step - 1]
    den = den_ref[me_y, me_z]
    for i in range(zs - 1):
        arrived(dz_ref.at[i], dz_sem.at[i])
        den = den + dz_ref[i]
    den = jnp.broadcast_to(den, (8, LANES)).T[:, 0:1]
    mine = num_ref[me_z, me_y, main]
    for i in range(zs - 1):
        arrived(rz_ref.at[i], rz_sem.at[i])
        mine = mine + rz_ref[i]
    targets_ref[0:104, :] = mine / den[0:104]
    targets_ref[104:128, :] = rest / den[104:128]


def shards(noise_latents, data_latents, projection):
    rows, width = noise_latents.shape
    cols = data_latents.shape[0]
    kdim = projection.shape[1]
    n_noise, n_dp = lax.axis_size("noise"), lax.axis_size("dp")
    ys, zs = ring_sizes(n_dp)
    rch, cch = rows // LANES, cols // LANES
    f32, bf16 = jnp.float32, jnp.bfloat16
    cfg = (rows, cols, n_noise, n_dp, kdim)
    dma = pltpu.SemaphoreType.DMA
    vmem = pl.BlockSpec(memory_space=pltpu.VMEM)
    targets, pot = pl.pallas_call(
        functools.partial(kernel, cfg),
        out_shape=(
            pltpu.VMEM((LANES, width), f32),
            pltpu.VMEM((cch, LANES), f32),
        ),
        in_specs=[pl.BlockSpec(memory_space=pl.ANY)] * 3,
        out_specs=(vmem, vmem),
        scratch_shapes=[
            pltpu.VMEM((rows, width), bf16),
            pltpu.VMEM((cols, width), bf16),
            pltpu.VMEM((kdim, width), bf16),
            pltpu.VMEM((rows, 256), bf16),
            pltpu.VMEM((cols, 256), bf16),
            pltpu.VMEM((zs, ys * LANES, cols), bf16),
            pltpu.VMEM((cols, 256), bf16),
            pltpu.VMEM((2 * kdim, width), bf16),
            pltpu.VMEM((rch, LANES), f32),
            pltpu.VMEM((cch, LANES), f32),
            pltpu.VMEM((n_noise, cch // 2, LANES), f32),
            pltpu.VMEM((n_noise, cch // 2, LANES), f32),
            pltpu.VMEM((rch, LANES), f32),
            pltpu.VMEM((rch, LANES), f32),
            pltpu.VMEM((rch, LANES), f32),
            pltpu.VMEM((rch, LANES), f32),
            pltpu.VMEM((ys, rch // 2, LANES), f32),
            pltpu.VMEM((ys, rch // 2, LANES), f32),
            pltpu.VMEM((zs, rch // 2, LANES), f32),
            pltpu.VMEM((zs, rch // 2, LANES), f32),
            pltpu.VMEM((n_noise, cch, LANES), f32),
            pltpu.VMEM((zs, ys, LANES, LANES), f32),
            pltpu.VMEM((zs, 104, LANES), f32),
            pltpu.VMEM((2, zs, 104, LANES), f32),
            pltpu.VMEM((zs - 1, 104, LANES), f32),
            pltpu.VMEM((zs - 1, ys, 24, LANES), f32),
            pltpu.VMEM((ys - 1, 24, LANES), f32),
            pltpu.VMEM((ys, zs, 1, LANES), f32),
            pltpu.VMEM((ys - 1, zs, 1, LANES), f32),
            pltpu.VMEM((zs - 1, 1, LANES), f32),
            dma((2, 2, n_noise)),
            dma((2, n_noise)),
            dma((2, 2, ys)),
            dma((2, 2, zs)),
            dma((zs, 2, 2)),
            dma((2, zs, 2, 2)),
            dma((zs - 1, 2)),
            dma((zs - 1, 2)),
            dma((ys - 1, 2)),
            dma((ys - 1, 2)),
            dma((zs - 1, 2)),
            dma((4,)),
        ],
        compiler_params=pltpu.CompilerParams(
            collective_id=0, has_side_effects=True, vmem_limit_bytes=56 * 2**20
        ),
        cost_estimate=pl.CostEstimate(
            flops=8 * rows * cols * 256, bytes_accessed=2**21, transcendentals=3 * rows * cols
        ),
    )(noise_latents, data_latents, projection.T)
    return (targets, pot.reshape(cols))


def solution(mesh):
    in_specs = (P("noise", None), P("dp", None), P())
    out_specs = (P(("noise", "dp"), None), P("dp"))
    return jax.shard_map(shards, mesh=mesh, in_specs=in_specs, out_specs=out_specs, check_vma=False)
```
